32 devices in a mesh: row: 4 (over y, x), col: 8 (over z, core).
Axes of the slice: x: 2, y: 2, z: 4, core: 2. Of those that a mesh axis runs over, the one named last changes fastest.
Arguments:
- inputs: bfloat16 [256, 8192], P('col', 'row'), may hold values from -6 to 6
- gate_weight: bfloat16 [8192, 28672], P('row', 'col'), may hold values from -0.0625 to 0.0625
- up_weight: bfloat16 [8192, 28672], P('row', 'col'), may hold values from -0.0625 to 0.0625
- down_weight: bfloat16 [28672, 8192], P('col', 'row'), may hold values from -0.03125 to 0.03125
- out_grad: bfloat16 [256, 8192], P('col', 'row'), may hold values from -1.5 to 1.5
Outputs:
- output: bfloat16 [256, 8192], P('col', 'row')
- in_grad: bfloat16 [256, 8192], P('col', 'row')
- gate_grad: bfloat16 [8192, 28672], P('row', 'col')
- up_grad: bfloat16 [8192, 28672], P('row', 'col')
- down_grad: bfloat16 [28672, 8192], P('col', 'row')
The draws below stay inside these ranges and needn't reach their ends.
All inputs are finite; a program needn't handle non-finite values.
Results may differ from the reference program's by a relative error of at most 0.005.
Values may be sent and summed in bfloat16 or wider, within the bound.
A program may use at most 192 MiB of HBM per device.

```python
import jax
import jax.numpy as jnp
from jax import lax

D = 8192
FF = 28672
TOKENS = 256


def levels(key, dims, shards, low, largest):
    gain, own = 1.0, jax.random.fold_in(key, 6)
    for position, blocks in shards:
        heights = jnp.exp(jax.random.uniform(jax.random.fold_in(own, position), (blocks,), jnp.float32, low / len(shards), largest / len(shards)))
        gain = gain * jnp.repeat(heights, dims[position] // blocks).reshape([-1 if axis == position else 1 for axis in range(len(dims))])
    return gain


def normal_values(stream_key, dims, deviation, reach, pieces=(), held_as=jnp.bfloat16):
    values = deviation * jax.random.normal(stream_key, dims, jnp.float32)
    if pieces:
        values = values * levels(stream_key, dims, pieces, -0.22, 0.18)
    return jnp.clip(values, -reach, reach).astype(held_as)


def setup_inputs(seed: int = 0) -> dict:
    key_list = jax.random.split(jax.random.key(seed), 6)
    inputs = normal_values(key_list[0], (TOKENS, D), 1.0, 6.0, ((0, 8), (1, 4)))
    gate_weight = normal_values(key_list[1], (D, FF), D ** -0.5, 0.0625, ((0, 4), (1, 8)))
    up_weight = normal_values(key_list[2], (D, FF), D ** -0.5, 0.0625, ((0, 4), (1, 8)))
    down_weight = normal_values(key_list[3], (FF, D), FF ** -0.5, 0.03125, ((0, 8), (1, 4)))
    out_grad = normal_values(key_list[4], (TOKENS, D), 0.25, 1.5, ((0, 8), (1, 4)))
    return {"inputs": inputs, "gate_weight": gate_weight, "up_weight": up_weight, "down_weight": down_weight, "out_grad": out_grad}


def contract_first(left, right):
    return lax.dot_general(left, right, (((0,), (0,)), ((), ())), preferred_element_type=jnp.float32)


def contract_last(left, right):
    return lax.dot_general(left, right, (((1,), (1,)), ((), ())), preferred_element_type=jnp.float32)


def reference(inputs, gate_weight, up_weight, down_weight, out_grad):
    gate_value = jnp.dot(inputs, gate_weight, preferred_element_type=jnp.float32)
    up_value = jnp.dot(inputs, up_weight, preferred_element_type=jnp.float32)
    sigmoid_gate = jax.nn.sigmoid(gate_value)
    hidden = (gate_value * sigmoid_gate * up_value).astype(jnp.bfloat16)
    output = jnp.dot(hidden, down_weight, preferred_element_type=jnp.float32).astype(jnp.bfloat16)
    hidden_grad = contract_last(out_grad, down_weight)
    slope = sigmoid_gate * (1.0 + gate_value * (1.0 - sigmoid_gate))
    gate_part = (hidden_grad * up_value * slope).astype(jnp.bfloat16)
    up_part = (hidden_grad * gate_value * sigmoid_gate).astype(jnp.bfloat16)
    in_grad = (contract_last(gate_part, gate_weight) + contract_last(up_part, up_weight)).astype(jnp.bfloat16)
    gate_grad = contract_first(inputs, gate_part).astype(jnp.bfloat16)
    up_grad = contract_first(inputs, up_part).astype(jnp.bfloat16)
    down_grad = contract_first(hidden, out_grad).astype(jnp.bfloat16)
    return output, in_grad, gate_grad, up_grad, down_grad
```

```python
import functools
import math

import jax
import jax.numpy as jnp
from jax import lax
from jax.experimental import pallas as pl
from jax.experimental.pallas import tpu as pltpu
from jax.sharding import PartitionSpec as P

MESH = pl.DeviceIdType.MESH
RING = 4
LAG = 2


def contract_first(left, right):
    return lax.dot_general(
        left, right, (((0,), (0,)), ((), ())), preferred_element_type=jnp.float32
    )


def contract_last(left, right):
    return lax.dot_general(
        left, right, (((1,), (1,)), ((), ())), preferred_element_type=jnp.float32
    )


def units_of(hidden_block):
    for units in (14, 28, 2):
        if hidden_block % (units * 128) == 0:
            return units
    return 2


def mix_kernel(
    side, planes, units,
    x_ref, og_ref, wg_ref, wu_ref, wd_ref,
    x_out, og_out, h_out, gp_out, up_out, acc_out, acc_in,
    xf, of, wgu, wdn, p_gu, p_h, own_gu, own_h, r1_gu, r1_h, p2_gu, p2_h, r2_gu, r2_h,
    full, stage, tmp,
    gz_send, gz_recv, gs_send, gs_recv,
    rs_send, rs_recv, ld_gu, ld_d, io_sem, st_sem,
):
    n, unit = side, wgu.shape[-1]
    owners = n * n
    tokens, width = xf.shape
    token_block = tokens // owners
    share = tokens // (2 * planes)
    pairs = units // 2
    row, col = lax.axis_index("row"), lax.axis_index("col")
    my_y, my_x = row // n, row % n
    z, core = col // 2, col % 2
    sibling = (row, z * 2 + (1 - core))

    def along_x(m):
        return (my_y * n + m, col)

    def along_y(m):
        return (m * n + my_x, col)

    firsts = ((my_x, along_x, my_y, along_y), (my_y, along_y, my_x, along_x))

    def slot_of(par, owner):
        oy, ox = owner // n, owner % n
        return ox * n + oy if par == 0 else oy * n + ox

    def plane(d):
        return (z + d) % planes

    partners = [sibling]
    for d in range(1, planes):
        partners.append((row, plane(d) * 2 + core))
    for d in range(1, n):
        partners.append(along_x((my_x + d) % n))
        partners.append(along_y((my_y + d) % n))
    barrier = pltpu.get_barrier_semaphore()
    for partner in partners:
        pl.semaphore_signal(barrier, inc=1, device_id=partner, device_id_type=MESH)

    def columns(k):
        return pl.ds(pl.multiple_of((k % units) * unit, 128), unit)

    def load_gu(k):
        s = k % RING
        return [
            pltpu.make_async_copy(ref.at[:, columns(k)], wgu.at[s, a], ld_gu.at[s, a])
            for a, ref in enumerate((wg_ref, wu_ref))
        ]

    def load_d(k):
        s = k % RING
        return [pltpu.make_async_copy(wd_ref.at[columns(k), :], wdn.at[s], ld_d.at[s])]

    def start(copies):
        for copy in copies:
            copy.start()

    def wait(copies):
        for copy in copies:
            copy.wait()

    for k in range(RING):
        start(load_gu(k))
        start(load_d(k))

    def rows(c):
        return pl.ds(pl.multiple_of(c * share, 16), share)

    def gather_z(a, src, dst, d):
        return pltpu.make_async_remote_copy(
            src_ref=src, dst_ref=dst.at[rows(col)],
            send_sem=gz_send.at[a, d - 1], recv_sem=gz_recv.at[a, d - 1],
            device_id=(row, plane(d) * 2 + core), device_id_type=MESH,
        )

    def gather_s(a, src, dst, d):
        c = ((z + planes - d) % planes) * 2 + core
        return pltpu.make_async_remote_copy(
            src_ref=src if d == 0 else dst.at[rows(c)], dst_ref=dst.at[rows(c)],
            send_sem=gs_send.at[a, d], recv_sem=gs_recv.at[a, d],
            device_id=sibling, device_id_type=MESH,
        )

    def gather_start(a, src, dst):
        for d in range(1, planes):
            gather_z(a, src, dst, d).start()
        gather_s(a, src, dst, 0).start()
        dst[rows(col), :] = src[...]

    def gather_end(a, src, dst):
        for d in range(1, planes):
            gather_z(a, src, dst, d).wait_recv()
            gather_s(a, src, dst, d).start()
        for d in range(planes):
            gather_s(a, src, dst, d).wait_recv()

    def gather_drain(a, src, dst):
        for d in range(1, planes):
            gather_z(a, src, dst, d).wait_send()
        for d in range(planes):
            gather_s(a, src, dst, d).wait_send()

    def first_send(kind, par, i, d):
        mine, line, _, _ = firsts[par]
        to = (mine + d) % n
        src, dst = ((p_gu, r1_gu), (p_h, r1_h))[kind]
        return pltpu.make_async_remote_copy(
            src_ref=src.at[i, pl.ds(to * n, n)], dst_ref=dst.at[i, d - 1],
            send_sem=rs_send.at[2 * kind, i, d - 1], recv_sem=rs_recv.at[2 * kind, i, d - 1],
            device_id=line(to), device_id_type=MESH,
        )

    def second_send(kind, par, i, d):
        _, _, mine, line = firsts[par]
        src, dst = ((p2_gu, r2_gu), (p2_h, r2_h))[kind]
        return pltpu.make_async_remote_copy(
            src_ref=src.at[i, d - 1], dst_ref=dst.at[i, d - 1],
            send_sem=rs_send.at[2 * kind + 1, i, d - 1],
            recv_sem=rs_recv.at[2 * kind + 1, i, d - 1],
            device_id=line((mine + d) % n), device_id_type=MESH,
        )

    def spread_first(par, i, d):
        mine_f, _, mine_s, line = firsts[par]
        block = full.at[i, mine_f * n + mine_s]
        return pltpu.make_async_remote_copy(
            src_ref=block, dst_ref=block,
            send_sem=rs_send.at[4, i, d - 1], recv_sem=rs_recv.at[4, i, d - 1],
            device_id=line((mine_s + d) % n), device_id_type=MESH,
        )

    def spread_second(par, i, d):
        mine, line, _, _ = firsts[par]
        blocks = full.at[i, pl.ds(mine * n, n)]
        return pltpu.make_async_remote_copy(
            src_ref=blocks, dst_ref=blocks,
            send_sem=rs_send.at[5, i, d - 1], recv_sem=rs_recv.at[5, i, d - 1],
            device_id=line((mine + d) % n), device_id_type=MESH,
        )

    def put_partial(par, i, a, value, partial, own, arrays):
        mine = firsts[par][0]
        for owner in range(owners):
            block = value[owner * token_block:(owner + 1) * token_block]
            tmp[a, slot_of(par, owner)] = block
            partial[i, slot_of(par, owner), a] = block.astype(jnp.bfloat16)
        for s in range(n):
            own[i, s, a] = tmp[a, mine * n + s]

    def project(par, i):
        s = i % RING
        wait(load_gu(i))
        for a in range(2):
            value = jnp.dot(xf[...], wgu[s, a], preferred_element_type=jnp.float32)
            put_partial(par, i, a, value, p_gu, own_gu, 2)
        start(load_gu(i + RING))
        for d in range(1, n):
            first_send(0, par, i, d).start()

    def project_grad(par, i):
        s = i % RING
        wait(load_d(i))
        value = contract_last(of[...], wdn[s])
        put_partial(par, i, 0, value, p_h, own_h, 1)
        start(load_d(i + RING))
        for d in range(1, n):
            first_send(1, par, i, d).start()

    def halfway(kind, par, i):
        mine = firsts[par][2]
        own, got, out = ((own_gu, r1_gu, p2_gu), (own_h, r1_h, p2_h))[kind]
        for d in range(1, n):
            first_send(kind, par, i, d).wait_recv()
        for d in range(1, n):
            s = (mine + d) % n
            for a in range(2 - kind):
                total = own[i, s, a]
                for e in range(n - 1):
                    total = total + got[i, e, s, a].astype(jnp.float32)
                out[i, d - 1, a] = total.astype(jnp.bfloat16)
            second_send(kind, par, i, d).start()

    def total_of(kind, par, i, a):
        mine = firsts[par][2]
        own, got, last = ((own_gu, r1_gu, r2_gu), (own_h, r1_h, r2_h))[kind]
        total = own[i, mine, a]
        for e in range(n - 1):
            total = total + got[i, e, mine, a].astype(jnp.float32)
        for e in range(n - 1):
            total = total + last[i, e, a].astype(jnp.float32)
        return total

    def gate(par, i):
        for kind in range(2):
            for d in range(1, n):
                second_send(kind, par, i, d).wait_recv()
        gate_value = total_of(0, par, i, 0)
        up_value = total_of(0, par, i, 1)
        hidden_grad = total_of(1, par, i, 0)
        sig = jax.nn.sigmoid(gate_value)
        mine = firsts[par][0] * n + firsts[par][2]
        full[i, mine, 0] = (gate_value * sig * up_value).astype(jnp.bfloat16)
        slope = sig * (1.0 + gate_value * (1.0 - sig))
        full[i, mine, 1] = (hidden_grad * up_value * slope).astype(jnp.bfloat16)
        full[i, mine, 2] = (hidden_grad * gate_value * sig).astype(jnp.bfloat16)
        for d in range(1, n):
            spread_first(par, i, d).start()

    def forward(par, i):
        for d in range(1, n):
            spread_first(par, i, d).wait_recv()
        for d in range(1, n):
            spread_second(par, i, d).start()

    def store(i):
        return [
            pltpu.make_async_copy(
                stage.at[a, :, columns(i)], out.at[:, columns(i)], st_sem.at[a, i]
            )
            for a, out in enumerate((h_out, gp_out, up_out))
        ]

    tile = min(512, width)

    def finish(par, i):
        k = units + i
        s = k % RING
        for d in range(1, n):
            spread_second(par, i, d).wait_recv()
        for a in range(3):
            for owner in range(owners):
                stage[a, pl.ds(owner * token_block, token_block), columns(i)] = full[
                    i, slot_of(par, owner), a
                ]
        start(store(i))
        wait(load_gu(k))
        wait(load_d(k))

        def add(t, carry):
            cols = pl.ds(pl.multiple_of(t * tile, 128), tile)
            acc_out[:, cols] += jnp.dot(
                stage[0, :, columns(i)], wdn[s, :, cols], preferred_element_type=jnp.float32
            )
            acc_in[:, cols] += contract_last(
                stage[1, :, columns(i)], wgu[s, 0, cols, :]
            ) + contract_last(stage[2, :, columns(i)], wgu[s, 1, cols, :])
            return carry

        lax.fori_loop(0, width // tile, add, 0)

        @pl.when(k + RING < 2 * units)
        def _():
            start(load_gu(k + RING))
            start(load_d(k + RING))

    pl.semaphore_wait(barrier, len(partners))
    gather_start(0, x_ref, xf)
    acc_out[...] = jnp.zeros_like(acc_out)
    acc_in[...] = jnp.zeros_like(acc_in)
    gather_end(0, x_ref, xf)
    gather_start(1, og_ref, of)

    starts = {}
    starts["project"] = 0
    starts["halfway0"] = LAG
    starts["grad"] = pairs
    starts["halfway1"] = pairs + LAG
    starts["gate"] = pairs + 2 * LAG
    starts["forward"] = pairs + 3 * LAG
    starts["finish"] = pairs + 4 * LAG
    steps = pairs + 4 * LAG + pairs

    def step(t, carry):
        def during(name, work):
            first = starts[name]

            @pl.when(jnp.logical_and(t >= first, t < first + pairs))
            def _():
                for par in range(2):
                    work(par, 2 * (t - first) + par)

        @pl.when(t == pairs)
        def _():
            gather_end(1, og_ref, of)

        during("project", project)
        during("grad", project_grad)
        during("halfway0", functools.partial(halfway, 0))
        during("halfway1", functools.partial(halfway, 1))
        during("gate", gate)
        during("forward", forward)
        during("finish", finish)
        return carry

    lax.fori_loop(0, steps, step, 0)

    outs = [
        pltpu.make_async_copy(xf, x_out, io_sem.at[0]),
        pltpu.make_async_copy(of, og_out, io_sem.at[1]),
    ]
    start(outs)

    def drain(p, carry):
        for par in range(2):
            i = 2 * p + par
            for d in range(1, n):
                for kind in range(2):
                    first_send(kind, par, i, d).wait_send()
                    second_send(kind, par, i, d).wait_send()
                spread_first(par, i, d).wait_send()
                spread_second(par, i, d).wait_send()
            wait(store(i))
        return carry

    lax.fori_loop(0, pairs, drain, 0)
    gather_drain(0, x_ref, xf)
    gather_drain(1, og_ref, of)
    wait(outs)


def mix(mesh, inputs, gate_weight, up_weight, down_weight, out_grad):
    rows, cols = mesh.shape["row"], mesh.shape["col"]
    n = math.isqrt(rows)
    assert n * n == rows and cols % 2 == 0
    planes = cols // 2
    tokens, width = inputs.shape[0] * cols, inputs.shape[1]
    hidden = gate_weight.shape[1]
    units = units_of(hidden)
    u = hidden // units
    tb = tokens // rows
    bf, f32 = jnp.bfloat16, jnp.float32
    dma = pltpu.SemaphoreType.DMA
    vmem = pl.BlockSpec(memory_space=pltpu.VMEM)
    hbm = pl.BlockSpec(memory_space=pl.ANY)
    flops = 12 * tokens * width * hidden
    return pl.pallas_call(
        functools.partial(mix_kernel, n, planes, units),
        out_shape=(
            jax.ShapeDtypeStruct((tokens, width), bf),
            jax.ShapeDtypeStruct((tokens, width), bf),
            jax.ShapeDtypeStruct((tokens, hidden), bf),
            jax.ShapeDtypeStruct((tokens, hidden), bf),
            jax.ShapeDtypeStruct((tokens, hidden), bf),
            jax.ShapeDtypeStruct((tokens, width), f32),
            jax.ShapeDtypeStruct((tokens, width), f32),
        ),
        in_specs=[vmem, vmem, hbm, hbm, hbm],
        out_specs=(hbm, hbm, hbm, hbm, hbm, vmem, vmem),
        scratch_shapes=[
            pltpu.VMEM((tokens, width), bf),
            pltpu.VMEM((tokens, width), bf),
            pltpu.VMEM((RING, 2, width, u), bf),
            pltpu.VMEM((RING, u, width), bf),
            pltpu.VMEM((units, rows, 2, tb, u), bf),
            pltpu.VMEM((units, rows, 1, tb, u), bf),
            pltpu.VMEM((units, n, 2, tb, u), f32),
            pltpu.VMEM((units, n, 1, tb, u), f32),
            pltpu.VMEM((units, n - 1, n, 2, tb, u), bf),
            pltpu.VMEM((units, n - 1, n, 1, tb, u), bf),
            pltpu.VMEM((units, n - 1, 2, tb, u), bf),
            pltpu.VMEM((units, n - 1, 1, tb, u), bf),
            pltpu.VMEM((units, n - 1, 2, tb, u), bf),
            pltpu.VMEM((units, n - 1, 1, tb, u), bf),
            pltpu.VMEM((units, rows, 3, tb, u), bf),
            pltpu.VMEM((3, tokens, hidden), bf),
            pltpu.VMEM((2, rows, tb, u), f32),
            dma((2, planes - 1)),
            dma((2, planes - 1)),
            dma((2, planes)),
            dma((2, planes)),
            dma((6, units, n - 1)),
            dma((6, units, n - 1)),
            dma((RING, 2)),
            dma((RING,)),
            dma((2,)),
            dma((3, units)),
        ],
        compiler_params=pltpu.CompilerParams(
            collective_id=0, has_side_effects=True, vmem_limit_bytes=60 * 2**20
        ),
        cost_estimate=pl.CostEstimate(
            flops=flops, bytes_accessed=12 * width * hidden, transcendentals=0
        ),
    )(inputs, out_grad, gate_weight, up_weight, down_weight)


def on_device(mesh, inputs, gate_weight, up_weight, down_weight, out_grad):
    all_inputs, all_grads, hidden, gate_part, up_part, out_sum, in_sum = mix(
        mesh, inputs, gate_weight, up_weight, down_weight, out_grad
    )
    scatter = functools.partial(
        lax.psum_scatter, axis_name="col", scatter_dimension=0, tiled=True
    )
    output = scatter(out_sum).astype(jnp.bfloat16)
    in_grad = scatter(in_sum).astype(jnp.bfloat16)
    gate_grad = contract_first(all_inputs, gate_part).astype(jnp.bfloat16)
    up_grad = contract_first(all_inputs, up_part).astype(jnp.bfloat16)
    down_grad = contract_first(hidden, all_grads).astype(jnp.bfloat16)
    return (output, in_grad, gate_grad, up_grad, down_grad)


def solution(mesh):
    in_specs = (P("col", "row"), P("row", "col"), P("row", "col"), P("col", "row"), P("col", "row"))
    out_specs = (
        P("col", "row"),
        P("col", "row"),
        P("row", "col"),
        P("row", "col"),
        P("col", "row"),
    )
    return jax.shard_map(
        functools.partial(on_device, mesh),
        mesh=mesh, in_specs=in_specs, out_specs=out_specs, check_vma=False,
    )
```

```python
import functools
import math

import jax
import jax.numpy as jnp
from jax import lax
from jax.experimental import pallas as pl
from jax.experimental.pallas import tpu as pltpu
from jax.sharding import PartitionSpec as P

MESH = pl.DeviceIdType.MESH
RING = 4
LAG = 2


def contract_first(left, right):
    return lax.dot_general(
        left, right, (((0,), (0,)), ((), ())), preferred_element_type=jnp.float32
    )


def contract_last(left, right):
    return lax.dot_general(
        left, right, (((1,), (1,)), ((), ())), preferred_element_type=jnp.float32
    )


def units_of(hidden_block):
    for units in (14, 28, 2):
        if hidden_block % (units * 128) == 0:
            return units
    return 2


def mix_kernel(
    side, planes, units,
    x_ref, og_ref, wg_ref, wu_ref, wd_ref,
    x_out, og_out, h_out, gp_out, up_out, keep, *rest,
):
    parts = rest[: planes - 1]
    (xf, of, wgu, wdn, p_gu, p_h, own_gu, own_h, r1_gu, r1_h, p2_gu, p2_h, r2_gu, r2_h,
    full, stage, tmp, acc_out, acc_in, pair_send, pair_recv,
    gz_send, gz_recv, gs_send, gs_recv,
    rs_send, rs_recv, ld_gu, ld_d, io_sem, st_sem, pr_send, pr_recv) = rest[planes - 1 :]
    n, unit = side, wgu.shape[-1]
    owners = n * n
    tokens, width = xf.shape
    token_block = tokens // owners
    share = tokens // (2 * planes)
    pairs = units // 2
    row, col = lax.axis_index("row"), lax.axis_index("col")
    my_y, my_x = row // n, row % n
    z, core = col // 2, col % 2
    sibling = (row, z * 2 + (1 - core))

    def along_x(m):
        return (my_y * n + m, col)

    def along_y(m):
        return (m * n + my_x, col)

    firsts = ((my_x, along_x, my_y, along_y), (my_y, along_y, my_x, along_x))

    def slot_of(par, owner):
        oy, ox = owner // n, owner % n
        return ox * n + oy if par == 0 else oy * n + ox

    def plane(d):
        return (z + d) % planes

    partners = [sibling]
    for d in range(1, planes):
        partners.append((row, plane(d) * 2 + core))
    for d in range(1, n):
        partners.append(along_x((my_x + d) % n))
        partners.append(along_y((my_y + d) % n))
    barrier = pltpu.get_barrier_semaphore()
    for partner in partners:
        pl.semaphore_signal(barrier, inc=1, device_id=partner, device_id_type=MESH)

    def columns(k):
        return pl.ds(pl.multiple_of((k % units) * unit, 128), unit)

    def load_gu(k):
        s = k % RING
        return [
            pltpu.make_async_copy(ref.at[:, columns(k)], wgu.at[s, a], ld_gu.at[s, a])
            for a, ref in enumerate((wg_ref, wu_ref))
        ]

    def load_d(k):
        s = k % RING
        return [pltpu.make_async_copy(wd_ref.at[columns(k), :], wdn.at[s], ld_d.at[s])]

    def start(copies):
        for copy in copies:
            copy.start()

    def wait(copies):
        for copy in copies:
            copy.wait()

    for k in range(RING):
        start(load_gu(k))
        start(load_d(k))

    def rows(c):
        return pl.ds(pl.multiple_of(c * share, 16), share)

    def gather_z(a, src, dst, d):
        return pltpu.make_async_remote_copy(
            src_ref=src, dst_ref=dst.at[rows(col)],
            send_sem=gz_send.at[a, d - 1], recv_sem=gz_recv.at[a, d - 1],
            device_id=(row, plane(d) * 2 + core), device_id_type=MESH,
        )

    def gather_s(a, src, dst, d):
        c = ((z + planes - d) % planes) * 2 + core
        return pltpu.make_async_remote_copy(
            src_ref=src if d == 0 else dst.at[rows(c)], dst_ref=dst.at[rows(c)],
            send_sem=gs_send.at[a, d], recv_sem=gs_recv.at[a, d],
            device_id=sibling, device_id_type=MESH,
        )

    def gather_start(a, src, dst):
        for d in range(1, planes):
            gather_z(a, src, dst, d).start()
        gather_s(a, src, dst, 0).start()
        dst[rows(col), :] = src[...]

    def gather_end(a, src, dst):
        for d in range(1, planes):
            gather_z(a, src, dst, d).wait_recv()
            gather_s(a, src, dst, d).start()
        for d in range(planes):
            gather_s(a, src, dst, d).wait_recv()

    def gather_drain(a, src, dst):
        for d in range(1, planes):
            gather_z(a, src, dst, d).wait_send()
        for d in range(planes):
            gather_s(a, src, dst, d).wait_send()

    def first_send(kind, par, i, d):
        mine, line, _, _ = firsts[par]
        to = (mine + d) % n
        src, dst = ((p_gu, r1_gu), (p_h, r1_h))[kind]
        return pltpu.make_async_remote_copy(
            src_ref=src.at[i, pl.ds(to * n, n)], dst_ref=dst.at[i, d - 1],
            send_sem=rs_send.at[2 * kind, i, d - 1], recv_sem=rs_recv.at[2 * kind, i, d - 1],
            device_id=line(to), device_id_type=MESH,
        )

    def second_send(kind, par, i, d):
        _, _, mine, line = firsts[par]
        src, dst = ((p2_gu, r2_gu), (p2_h, r2_h))[kind]
        return pltpu.make_async_remote_copy(
            src_ref=src.at[i, d - 1], dst_ref=dst.at[i, d - 1],
            send_sem=rs_send.at[2 * kind + 1, i, d - 1],
            recv_sem=rs_recv.at[2 * kind + 1, i, d - 1],
            device_id=line((mine + d) % n), device_id_type=MESH,
        )

    def spread_first(par, i, d):
        mine_f, _, mine_s, line = firsts[par]
        block = full.at[i, mine_f * n + mine_s]
        return pltpu.make_async_remote_copy(
            src_ref=block, dst_ref=block,
            send_sem=rs_send.at[4, i, d - 1], recv_sem=rs_recv.at[4, i, d - 1],
            device_id=line((mine_s + d) % n), device_id_type=MESH,
        )

    def spread_second(par, i, d):
        mine, line, _, _ = firsts[par]
        blocks = full.at[i, pl.ds(mine * n, n)]
        return pltpu.make_async_remote_copy(
            src_ref=blocks, dst_ref=blocks,
            send_sem=rs_send.at[5, i, d - 1], recv_sem=rs_recv.at[5, i, d - 1],
            device_id=line((mine + d) % n), device_id_type=MESH,
        )

    def put_partial(par, i, a, value, partial, own, arrays):
        mine = firsts[par][0]
        for owner in range(owners):
            block = value[owner * token_block:(owner + 1) * token_block]
            tmp[a, slot_of(par, owner)] = block
            partial[i, slot_of(par, owner), a] = block.astype(jnp.bfloat16)
        for s in range(n):
            own[i, s, a] = tmp[a, mine * n + s]

    def project(par, i):
        s = i % RING
        wait(load_gu(i))
        for a in range(2):
            value = jnp.dot(xf[...], wgu[s, a], preferred_element_type=jnp.float32)
            put_partial(par, i, a, value, p_gu, own_gu, 2)
        start(load_gu(i + RING))
        for d in range(1, n):
            first_send(0, par, i, d).start()

    def project_grad(par, i):
        s = i % RING
        wait(load_d(i))
        value = contract_last(of[...], wdn[s])
        put_partial(par, i, 0, value, p_h, own_h, 1)
        start(load_d(i + RING))
        for d in range(1, n):
            first_send(1, par, i, d).start()

    def halfway(kind, par, i):
        mine = firsts[par][2]
        own, got, out = ((own_gu, r1_gu, p2_gu), (own_h, r1_h, p2_h))[kind]
        for d in range(1, n):
            first_send(kind, par, i, d).wait_recv()
        for d in range(1, n):
            s = (mine + d) % n
            for a in range(2 - kind):
                total = own[i, s, a]
                for e in range(n - 1):
                    total = total + got[i, e, s, a].astype(jnp.float32)
                out[i, d - 1, a] = total.astype(jnp.bfloat16)
            second_send(kind, par, i, d).start()

    def total_of(kind, par, i, a):
        mine = firsts[par][2]
        own, got, last = ((own_gu, r1_gu, r2_gu), (own_h, r1_h, r2_h))[kind]
        total = own[i, mine, a]
        for e in range(n - 1):
            total = total + got[i, e, mine, a].astype(jnp.float32)
        for e in range(n - 1):
            total = total + last[i, e, a].astype(jnp.float32)
        return total

    def gate(par, i):
        for kind in range(2):
            for d in range(1, n):
                second_send(kind, par, i, d).wait_recv()
        gate_value = total_of(0, par, i, 0)
        up_value = total_of(0, par, i, 1)
        hidden_grad = total_of(1, par, i, 0)
        sig = jax.nn.sigmoid(gate_value)
        mine = firsts[par][0] * n + firsts[par][2]
        full[i, mine, 0] = (gate_value * sig * up_value).astype(jnp.bfloat16)
        slope = sig * (1.0 + gate_value * (1.0 - sig))
        full[i, mine, 1] = (hidden_grad * up_value * slope).astype(jnp.bfloat16)
        full[i, mine, 2] = (hidden_grad * gate_value * sig).astype(jnp.bfloat16)
        for d in range(1, n):
            spread_first(par, i, d).start()

    def forward(par, i):
        for d in range(1, n):
            spread_first(par, i, d).wait_recv()
        for d in range(1, n):
            spread_second(par, i, d).start()

    def store(i):
        return [
            pltpu.make_async_copy(
                stage.at[a, :, columns(i)], out.at[:, columns(i)], st_sem.at[a, i]
            )
            for a, out in enumerate((h_out, gp_out, up_out))
        ]

    tile = min(512, width)

    def finish(pair):
        i = 2 * pair
        k = units + i
        s = k % RING
        for par in range(2):
            for d in range(1, n):
                spread_second(par, i + par, d).wait_recv()
            for a in range(3):
                for owner in range(owners):
                    stage[a, pl.ds(owner * token_block, token_block), columns(i + par)] = full[
                        i + par, slot_of(par, owner), a
                    ]
            start(store(i + par))
            wait(load_gu(k + par))
            wait(load_d(k + par))
        both = pl.ds(pl.multiple_of(i * unit, 128), 2 * unit)

        def add(t, carry):
            cols = pl.ds(pl.multiple_of(t * tile, 128), tile)
            down = wdn[pl.ds(s, 2), :, cols].reshape(2 * unit, tile)
            acc_out[:, cols] += jnp.dot(
                stage[0, :, both], down, preferred_element_type=jnp.float32
            )
            total = acc_in[:, cols]
            for par in range(2):
                for a in range(2):
                    total = total + contract_last(
                        stage[1 + a, :, columns(i + par)], wgu[s + par, a, cols, :]
                    )
            acc_in[:, cols] = total
            return carry

        lax.fori_loop(0, width // tile, add, 0)

        @pl.when(k + RING < 2 * units)
        def _():
            for par in range(2):
                start(load_gu(k + par + RING))
                start(load_d(k + par + RING))

    pl.semaphore_wait(barrier, len(partners))
    gather_start(0, x_ref, xf)
    acc_out[...] = jnp.zeros_like(acc_out)
    acc_in[...] = jnp.zeros_like(acc_in)
    gather_end(0, x_ref, xf)
    gather_start(1, og_ref, of)

    starts = {}
    starts["project"] = 0
    starts["halfway0"] = LAG
    starts["grad"] = pairs
    starts["halfway1"] = pairs + LAG
    starts["gate"] = pairs + 2 * LAG
    starts["forward"] = starts["gate"] + 1
    starts["finish"] = starts["gate"] + 2
    steps = starts["finish"] + pairs

    def step(t, carry):
        def during(name, work):
            first = starts[name]

            @pl.when(jnp.logical_and(t >= first, t < first + pairs))
            def _():
                for par in range(2):
                    work(par, 2 * (t - first) + par)

        @pl.when(t == pairs)
        def _():
            gather_end(1, og_ref, of)

        during("project", project)
        during("grad", project_grad)
        during("halfway0", functools.partial(halfway, 0))
        during("halfway1", functools.partial(halfway, 1))
        during("gate", gate)
        during("forward", forward)

        @pl.when(t >= starts["finish"])
        def _():
            finish(t - starts["finish"])

        return carry

    lax.fori_loop(0, steps, step, 0)

    totals = (acc_out, acc_in)

    def swap(a):
        return pltpu.make_async_remote_copy(
            src_ref=pair_send.at[a], dst_ref=pair_recv.at[a],
            send_sem=pr_send.at[a], recv_sem=pr_recv.at[a],
            device_id=sibling, device_id_type=MESH,
        )

    for a in range(2):
        for p in range(planes):
            pair_send[a, p] = totals[a][rows(2 * p + 1 - core), :].astype(jnp.bfloat16)
        swap(a).start()
    for a in range(2):
        swap(a).wait_recv()
        for d in range(planes):
            p = plane(d)
            value = totals[a][rows(2 * p + core), :] + pair_recv[a, p].astype(jnp.float32)
            if d == 0:
                keep[a] = value
            else:
                parts[d - 1][a] = value.astype(jnp.bfloat16)

    outs = [
        pltpu.make_async_copy(xf, x_out, io_sem.at[0]),
        pltpu.make_async_copy(of, og_out, io_sem.at[1]),
    ]
    start(outs)

    def drain(p, carry):
        for par in range(2):
            i = 2 * p + par
            for d in range(1, n):
                for kind in range(2):
                    first_send(kind, par, i, d).wait_send()
                    second_send(kind, par, i, d).wait_send()
                spread_first(par, i, d).wait_send()
                spread_second(par, i, d).wait_send()
            wait(store(i))
        return carry

    lax.fori_loop(0, pairs, drain, 0)
    gather_drain(0, x_ref, xf)
    gather_drain(1, og_ref, of)
    wait(outs)
    for a in range(2):
        swap(a).wait_send()


def mix(mesh, inputs, gate_weight, up_weight, down_weight, out_grad):
    rows, cols = mesh.shape["row"], mesh.shape["col"]
    n = math.isqrt(rows)
    assert n * n == rows and cols % 2 == 0
    planes = cols // 2
    tokens, width = inputs.shape[0] * cols, inputs.shape[1]
    hidden = gate_weight.shape[1]
    units = units_of(hidden)
    u = hidden // units
    tb = tokens // rows
    share = tokens // cols
    bf, f32 = jnp.bfloat16, jnp.float32
    dma = pltpu.SemaphoreType.DMA
    vmem = pl.BlockSpec(memory_space=pltpu.VMEM)
    hbm = pl.BlockSpec(memory_space=pl.ANY)
    flops = 12 * tokens * width * hidden
    return pl.pallas_call(
        functools.partial(mix_kernel, n, planes, units),
        out_shape=(
            jax.ShapeDtypeStruct((tokens, width), bf),
            jax.ShapeDtypeStruct((tokens, width), bf),
            jax.ShapeDtypeStruct((tokens, hidden), bf),
            jax.ShapeDtypeStruct((tokens, hidden), bf),
            jax.ShapeDtypeStruct((tokens, hidden), bf),
            jax.ShapeDtypeStruct((2, share, width), f32),
        )
        + (jax.ShapeDtypeStruct((2, share, width), bf),) * (planes - 1),
        in_specs=[vmem, vmem, hbm, hbm, hbm],
        out_specs=(hbm, hbm, hbm, hbm, hbm, vmem) + (vmem,) * (planes - 1),
        scratch_shapes=[
            pltpu.VMEM((tokens, width), bf),
            pltpu.VMEM((tokens, width), bf),
            pltpu.VMEM((RING, 2, width, u), bf),
            pltpu.VMEM((RING, u, width), bf),
            pltpu.VMEM((units, rows, 2, tb, u), bf),
            pltpu.VMEM((units, rows, 1, tb, u), bf),
            pltpu.VMEM((units, n, 2, tb, u), f32),
            pltpu.VMEM((units, n, 1, tb, u), f32),
            pltpu.VMEM((units, n - 1, n, 2, tb, u), bf),
            pltpu.VMEM((units, n - 1, n, 1, tb, u), bf),
            pltpu.VMEM((units, n - 1, 2, tb, u), bf),
            pltpu.VMEM((units, n - 1, 1, tb, u), bf),
            pltpu.VMEM((units, n - 1, 2, tb, u), bf),
            pltpu.VMEM((units, n - 1, 1, tb, u), bf),
            pltpu.VMEM((units, rows, 3, tb, u), bf),
            pltpu.VMEM((3, tokens, hidden), bf),
            pltpu.VMEM((2, rows, tb, u), f32),
            pltpu.VMEM((tokens, width), f32),
            pltpu.VMEM((tokens, width), f32),
            pltpu.VMEM((2, planes, share, width), bf),
            pltpu.VMEM((2, planes, share, width), bf),
            dma((2, planes - 1)),
            dma((2, planes - 1)),
            dma((2, planes)),
            dma((2, planes)),
            dma((6, units, n - 1)),
            dma((6, units, n - 1)),
            dma((RING, 2)),
            dma((RING,)),
            dma((2,)),
            dma((3, units)),
            dma((2,)),
            dma((2,)),
        ],
        compiler_params=pltpu.CompilerParams(
            collective_id=0, has_side_effects=True, vmem_limit_bytes=60 * 2**20
        ),
        cost_estimate=pl.CostEstimate(
            flops=flops, bytes_accessed=12 * width * hidden, transcendentals=0
        ),
    )(inputs, out_grad, gate_weight, up_weight, down_weight)


def grads_kernel(first, x_ref, gp_ref, up_ref, h_ref, og_ref, gate_ref, up_out, down_ref):
    step = pl.program_id(0)

    def fill(left, right, out):
        columns = out.shape[1]
        tile = 512 if columns % 512 == 0 else 256
        for t in range(columns // tile):
            cols = slice(t * tile, (t + 1) * tile)
            out[:, cols] = jnp.dot(
                left, right[:, cols], preferred_element_type=jnp.float32
            ).astype(out.dtype)

    @pl.when(step < first)
    def _():
        left = x_ref[...].T
        fill(left, gp_ref, gate_ref)
        fill(left, up_ref, up_out)

    @pl.when(step >= first)
    def _():
        fill(h_ref[...].T, og_ref, down_ref)


def weight_grads(inputs, gate_part, up_part, hidden, out_grad):
    tokens, width = inputs.shape
    units = hidden.shape[1]
    wide = 256
    tall = 512 if units % 512 == 0 else 256
    first, second = width // wide, units // tall
    bf = jnp.bfloat16
    whole = functools.partial(pl.BlockSpec, index_map=lambda i: (0, 0))
    return pl.pallas_call(
        functools.partial(grads_kernel, first),
        grid=(first + second,),
        out_shape=(
            jax.ShapeDtypeStruct((width, units), bf),
            jax.ShapeDtypeStruct((width, units), bf),
            jax.ShapeDtypeStruct((units, width), bf),
        ),
        in_specs=[
            pl.BlockSpec((tokens, wide), lambda i: (0, jnp.minimum(i, first - 1))),
            whole((tokens, units)),
            whole((tokens, units)),
            pl.BlockSpec((tokens, tall), lambda i: (0, jnp.maximum(i - first, 0))),
            whole((tokens, width)),
        ],
        out_specs=(
            pl.BlockSpec((wide, units), lambda i: (jnp.minimum(i, first - 1), 0)),
            pl.BlockSpec((wide, units), lambda i: (jnp.minimum(i, first - 1), 0)),
            pl.BlockSpec((tall, width), lambda i: (jnp.maximum(i - first, 0), 0)),
        ),
        compiler_params=pltpu.CompilerParams(vmem_limit_bytes=40 * 2**20),
        cost_estimate=pl.CostEstimate(
            flops=6 * tokens * width * units,
            bytes_accessed=6 * width * units,
            transcendentals=0,
        ),
    )(inputs, gate_part, up_part, hidden, out_grad)


def on_device(mesh, inputs, gate_weight, up_weight, down_weight, out_grad):
    all_inputs, all_grads, hidden, gate_part, up_part, keep, *parts = mix(
        mesh, inputs, gate_weight, up_weight, down_weight, out_grad
    )
    cols = mesh.shape["col"]
    arrived = [
        lax.ppermute(part, "col", [(c, (c + 2 * d + 2) % cols) for c in range(cols)])
        for d, part in enumerate(parts)
    ]
    gate_grad, up_grad, down_grad = weight_grads(
        all_inputs, gate_part, up_part, hidden, all_grads
    )
    total = keep
    for part in arrived:
        total = total + part.astype(jnp.float32)
    output, in_grad = total[0].astype(jnp.bfloat16), total[1].astype(jnp.bfloat16)
    return (output, in_grad, gate_grad, up_grad, down_grad)


def solution(mesh):
    in_specs = (P("col", "row"), P("row", "col"), P("row", "col"), P("col", "row"), P("col", "row"))
    out_specs = (
        P("col", "row"),
        P("col", "row"),
        P("row", "col"),
        P("row", "col"),
        P("col", "row"),
    )
    return jax.shard_map(
        functools.partial(on_device, mesh),
        mesh=mesh, in_specs=in_specs, out_specs=out_specs, check_vma=False,
    )
```

```python
import functools
import math

import jax
import jax.numpy as jnp
from jax import lax
from jax.experimental import pallas as pl
from jax.experimental.pallas import tpu as pltpu
from jax.sharding import PartitionSpec as P

MESH = pl.DeviceIdType.MESH
RING = 4
LAG = 2


def contract_first(left, right):
    return lax.dot_general(
        left, right, (((0,), (0,)), ((), ())), preferred_element_type=jnp.float32
    )


def contract_last(left, right):
    return lax.dot_general(
        left, right, (((1,), (1,)), ((), ())), preferred_element_type=jnp.float32
    )


def units_of(hidden_block):
    for units in (14, 28, 2):
        if hidden_block % (units * 128) == 0:
            return units
    return 2


def mix_kernel(
    side, planes, units,
    x_ref, og_ref, wg_ref, wu_ref, wd_ref,
    xt_out, og_out, ht_out, gp_out, up_out, output, keep, *rest,
):
    parts = rest[: planes - 1]
    (xf, of, wgu, wdn, p_gu, p_h, own_gu, own_h, r1_gu, r1_h, p2_gu, p2_h, r2_gu, r2_h,
    full_h, full_g, xt, ht, hp, stage, tmp, acc_out, acc_in, pair_send, pair_recv, z_out, z_in,
    gz_send, gz_recv, gs_send, gs_recv,
    rs_send, rs_recv, ld_gu, ld_d, io_sem, st_sem, pr_send, pr_recv, z_send, z_recv) = rest[planes - 1 :]
    n, unit = side, wgu.shape[-1]
    owners = n * n
    tokens, width = xf.shape
    token_block = tokens // owners
    share = tokens // (2 * planes)
    pairs = units // 2
    row, col = lax.axis_index("row"), lax.axis_index("col")
    my_y, my_x = row // n, row % n
    z, core = col // 2, col % 2
    sibling = (row, z * 2 + (1 - core))

    def along_x(m):
        return (my_y * n + m, col)

    def along_y(m):
        return (m * n + my_x, col)

    firsts = ((my_x, along_x, my_y, along_y), (my_y, along_y, my_x, along_x))

    def slot_of(par, owner):
        oy, ox = owner // n, owner % n
        return ox * n + oy if par == 0 else oy * n + ox

    def plane(d):
        return (z + d) % planes

    partners = [sibling]
    for d in range(1, planes):
        partners.append((row, plane(d) * 2 + core))
    for d in range(1, n):
        partners.append(along_x((my_x + d) % n))
        partners.append(along_y((my_y + d) % n))
    barrier = pltpu.get_barrier_semaphore()
    for partner in partners:
        pl.semaphore_signal(barrier, inc=1, device_id=partner, device_id_type=MESH)

    def columns(k):
        return pl.ds(pl.multiple_of((k % units) * unit, 128), unit)

    def load_gu(k):
        s = k % RING
        return [
            pltpu.make_async_copy(ref.at[:, columns(k)], wgu.at[s, a], ld_gu.at[s, a])
            for a, ref in enumerate((wg_ref, wu_ref))
        ]

    def load_d(k):
        s = k % RING
        return [pltpu.make_async_copy(wd_ref.at[columns(k), :], wdn.at[s], ld_d.at[s])]

    def start(copies):
        for copy in copies:
            copy.start()

    def wait(copies):
        for copy in copies:
            copy.wait()

    for k in range(RING):
        start(load_gu(k))
        start(load_d(k))

    def rows(c):
        return pl.ds(pl.multiple_of(c * share, 16), share)

    def gather_z(a, src, dst, d):
        return pltpu.make_async_remote_copy(
            src_ref=src, dst_ref=dst.at[rows(col)],
            send_sem=gz_send.at[a, d - 1], recv_sem=gz_recv.at[a, d - 1],
            device_id=(row, plane(d) * 2 + core), device_id_type=MESH,
        )

    def gather_s(a, src, dst, d):
        c = ((z + planes - d) % planes) * 2 + core
        return pltpu.make_async_remote_copy(
            src_ref=src if d == 0 else dst.at[rows(c)], dst_ref=dst.at[rows(c)],
            send_sem=gs_send.at[a, d], recv_sem=gs_recv.at[a, d],
            device_id=sibling, device_id_type=MESH,
        )

    def gather_start(a, src, dst):
        for d in range(1, planes):
            gather_z(a, src, dst, d).start()
        gather_s(a, src, dst, 0).start()
        dst[rows(col), :] = src[...]

    def gather_end(a, src, dst):
        for d in range(1, planes):
            gather_z(a, src, dst, d).wait_recv()
            gather_s(a, src, dst, d).start()
        for d in range(planes):
            gather_s(a, src, dst, d).wait_recv()

    def gather_drain(a, src, dst):
        for d in range(1, planes):
            gather_z(a, src, dst, d).wait_send()
        for d in range(planes):
            gather_s(a, src, dst, d).wait_send()

    def first_send(kind, par, i, d):
        mine, line, _, _ = firsts[par]
        to = (mine + d) % n
        src, dst = ((p_gu, r1_gu), (p_h, r1_h))[kind]
        return pltpu.make_async_remote_copy(
            src_ref=src.at[i, pl.ds(to * n, n)], dst_ref=dst.at[i, d - 1],
            send_sem=rs_send.at[2 * kind, i, d - 1], recv_sem=rs_recv.at[2 * kind, i, d - 1],
            device_id=line(to), device_id_type=MESH,
        )

    def second_send(kind, par, i, d):
        _, _, mine, line = firsts[par]
        src, dst = ((p2_gu, r2_gu), (p2_h, r2_h))[kind]
        return pltpu.make_async_remote_copy(
            src_ref=src.at[i, d - 1], dst_ref=dst.at[i, d - 1],
            send_sem=rs_send.at[2 * kind + 1, i, d - 1],
            recv_sem=rs_recv.at[2 * kind + 1, i, d - 1],
            device_id=line((mine + d) % n), device_id_type=MESH,
        )

    fulls = (full_h, full_g)

    def spread_first(kind, par, i, d):
        mine_f, _, mine_s, line = firsts[par]
        block = fulls[kind].at[i, mine_f * n + mine_s]
        return pltpu.make_async_remote_copy(
            src_ref=block, dst_ref=block,
            send_sem=rs_send.at[4 + 2 * kind, i, d - 1],
            recv_sem=rs_recv.at[4 + 2 * kind, i, d - 1],
            device_id=line((mine_s + d) % n), device_id_type=MESH,
        )

    def spread_second(kind, par, i, d):
        mine, line, _, _ = firsts[par]
        blocks = fulls[kind].at[i, pl.ds(mine * n, n)]
        return pltpu.make_async_remote_copy(
            src_ref=blocks, dst_ref=blocks,
            send_sem=rs_send.at[5 + 2 * kind, i, d - 1],
            recv_sem=rs_recv.at[5 + 2 * kind, i, d - 1],
            device_id=line((mine + d) % n), device_id_type=MESH,
        )

    def put_partial(par, i, a, value, partial, own, arrays):
        mine = firsts[par][0]
        for owner in range(owners):
            block = value[owner * token_block:(owner + 1) * token_block]
            tmp[a, slot_of(par, owner)] = block
            partial[i, slot_of(par, owner), a] = block.astype(jnp.bfloat16)
        for s in range(n):
            own[i, s, a] = tmp[a, mine * n + s]

    def project(par, i):
        s = i % RING
        wait(load_gu(i))
        for a in range(2):
            value = jnp.dot(xf[...], wgu[s, a], preferred_element_type=jnp.float32)
            put_partial(par, i, a, value, p_gu, own_gu, 2)
        start(load_gu(i + RING))
        for d in range(1, n):
            first_send(0, par, i, d).start()

    tile = min(512, width)

    def grad_pair(pair):
        i = 2 * pair
        s = i % RING
        for par in range(2):
            wait(load_d(i + par))
            value = contract_last(of[...], wdn[s + par])
            put_partial(par, i + par, 0, value, p_h, own_h, 1)
            for d in range(1, n):
                first_send(1, par, i + par, d).start()
        for par in range(2):
            for d in range(1, n):
                spread_second(0, par, i + par, d).wait_recv()
            for owner in range(owners):
                hp[pl.ds(owner * token_block, token_block), par * unit:(par + 1) * unit] = (
                    full_h[i + par, slot_of(par, owner), 0]
                )
        ht[pl.ds(pl.multiple_of(i * unit, 128), 2 * unit), :] = hp[...].T
        store_h(i).start()

        def add(t, carry):
            cols = pl.ds(pl.multiple_of(t * tile, 128), tile)
            down = wdn[pl.ds(s, 2), :, cols].reshape(2 * unit, tile)
            acc_out[:, cols] += jnp.dot(
                hp[...], down, preferred_element_type=jnp.float32
            )
            return carry

        lax.fori_loop(0, width // tile, add, 0)

        @pl.when(i + RING < units)
        def _():
            for par in range(2):
                start(load_d(i + par + RING))

    def halfway(kind, par, i):
        mine = firsts[par][2]
        own, got, out = ((own_gu, r1_gu, p2_gu), (own_h, r1_h, p2_h))[kind]
        for d in range(1, n):
            first_send(kind, par, i, d).wait_recv()
        for d in range(1, n):
            s = (mine + d) % n
            for a in range(2 - kind):
                total = own[i, s, a]
                for e in range(n - 1):
                    total = total + got[i, e, s, a].astype(jnp.float32)
                out[i, d - 1, a] = total.astype(jnp.bfloat16)
            second_send(kind, par, i, d).start()

    def total_of(kind, par, i, a):
        mine = firsts[par][2]
        own, got, last = ((own_gu, r1_gu, r2_gu), (own_h, r1_h, r2_h))[kind]
        total = own[i, mine, a]
        for e in range(n - 1):
            total = total + got[i, e, mine, a].astype(jnp.float32)
        for e in range(n - 1):
            total = total + last[i, e, a].astype(jnp.float32)
        return total

    def gate_hidden(par, i):
        for d in range(1, n):
            second_send(0, par, i, d).wait_recv()
        gate_value = total_of(0, par, i, 0)
        up_value = total_of(0, par, i, 1)
        sig = jax.nn.sigmoid(gate_value)
        mine = firsts[par][0] * n + firsts[par][2]
        full_h[i, mine, 0] = (gate_value * sig * up_value).astype(jnp.bfloat16)
        for d in range(1, n):
            spread_first(0, par, i, d).start()

    def gate_grads(par, i):
        for d in range(1, n):
            second_send(1, par, i, d).wait_recv()
        gate_value = total_of(0, par, i, 0)
        up_value = total_of(0, par, i, 1)
        hidden_grad = total_of(1, par, i, 0)
        sig = jax.nn.sigmoid(gate_value)
        mine = firsts[par][0] * n + firsts[par][2]
        slope = sig * (1.0 + gate_value * (1.0 - sig))
        full_g[i, mine, 0] = (hidden_grad * up_value * slope).astype(jnp.bfloat16)
        full_g[i, mine, 1] = (hidden_grad * gate_value * sig).astype(jnp.bfloat16)
        for d in range(1, n):
            spread_first(1, par, i, d).start()

    def forward(kind, par, i):
        for d in range(1, n):
            spread_first(kind, par, i, d).wait_recv()
        for d in range(1, n):
            spread_second(kind, par, i, d).start()

    def store_h(i):
        strip = pl.ds(pl.multiple_of(i * unit, 128), 2 * unit)
        return pltpu.make_async_copy(ht.at[strip], ht_out.at[strip], st_sem.at[2, i])

    def store(i):
        return [
            pltpu.make_async_copy(
                stage.at[a, :, columns(i)], out.at[:, columns(i)], st_sem.at[a, i]
            )
            for a, out in enumerate((gp_out, up_out))
        ]

    def finish(pair):
        i = 2 * pair
        k = units + i
        s = k % RING
        for par in range(2):
            for d in range(1, n):
                spread_second(1, par, i + par, d).wait_recv()
            for a in range(2):
                for owner in range(owners):
                    stage[a, pl.ds(owner * token_block, token_block), columns(i + par)] = full_g[
                        i + par, slot_of(par, owner), a
                    ]
            start(store(i + par))
            wait(load_gu(k + par))

        def add(t, carry):
            cols = pl.ds(pl.multiple_of(t * tile, 128), tile)
            total = acc_in[:, cols]
            for par in range(2):
                for a in range(2):
                    total = total + contract_last(
                        stage[a, :, columns(i + par)], wgu[s + par, a, cols, :]
                    )
            acc_in[:, cols] = total
            return carry

        lax.fori_loop(0, width // tile, add, 0)

        @pl.when(k + RING < 2 * units)
        def _():
            for par in range(2):
                start(load_gu(k + par + RING))

    totals = (acc_out, acc_in)

    def swap(a):
        return pltpu.make_async_remote_copy(
            src_ref=pair_send.at[a], dst_ref=pair_recv.at[a],
            send_sem=pr_send.at[a], recv_sem=pr_recv.at[a],
            device_id=sibling, device_id_type=MESH,
        )

    def swap_start(a):
        for p in range(planes):
            pair_send[a, p] = totals[a][rows(2 * p + 1 - core), :].astype(jnp.bfloat16)
        swap(a).start()

    def chip_sum(a, d):
        p = plane(d)
        return totals[a][rows(2 * p + core), :] + pair_recv[a, p].astype(jnp.float32)

    def z_copy(d):
        return pltpu.make_async_remote_copy(
            src_ref=z_out.at[d - 1], dst_ref=z_in.at[d - 1],
            send_sem=z_send.at[d - 1], recv_sem=z_recv.at[d - 1],
            device_id=(row, plane(d) * 2 + core), device_id_type=MESH,
        )

    def z_start():
        swap(0).wait_recv()
        for d in range(1, planes):
            z_out[d - 1] = chip_sum(0, d).astype(jnp.bfloat16)
            z_copy(d).start()

    def z_end():
        total = chip_sum(0, 0)
        for d in range(1, planes):
            z_copy(d).wait_recv()
            total = total + z_in[d - 1].astype(jnp.float32)
        output[...] = total

    pl.semaphore_wait(barrier, len(partners))
    gather_start(0, x_ref, xf)
    acc_out[...] = jnp.zeros_like(acc_out)
    acc_in[...] = jnp.zeros_like(acc_in)
    gather_end(0, x_ref, xf)
    gather_start(1, og_ref, of)

    starts = {}
    starts["project"] = 0
    starts["halfway0"] = LAG
    starts["hidden"] = 2 * LAG
    starts["spread0"] = 2 * LAG + 1
    starts["grad"] = pairs
    starts["halfway1"] = pairs + LAG
    starts["grads"] = pairs + 2 * LAG
    starts["spread1"] = starts["grads"] + 1
    starts["finish"] = starts["grads"] + 2
    steps = starts["finish"] + pairs

    def step(t, carry):
        def during(name, work):
            first = starts[name]

            @pl.when(jnp.logical_and(t >= first, t < first + pairs))
            def _():
                for par in range(2):
                    work(par, 2 * (t - first) + par)

        @pl.when(t == pairs)
        def _():
            gather_end(1, og_ref, of)
            for c in range(0, width, 256):
                xt[c:c + 256, :] = xf[:, c:c + 256].T

        during("project", project)
        during("halfway0", functools.partial(halfway, 0))
        during("hidden", gate_hidden)
        during("spread0", functools.partial(forward, 0))

        @pl.when(jnp.logical_and(t >= pairs, t < 2 * pairs))
        def _():
            grad_pair(t - pairs)

        during("halfway1", functools.partial(halfway, 1))
        during("grads", gate_grads)
        during("spread1", functools.partial(forward, 1))

        @pl.when(t == 2 * pairs)
        def _():
            swap_start(0)

        @pl.when(t == 2 * pairs + 1)
        def _():
            z_start()

        @pl.when(t >= starts["finish"])
        def _():
            finish(t - starts["finish"])

        return carry

    lax.fori_loop(0, steps, step, 0)

    swap_start(1)
    outs = [
        pltpu.make_async_copy(xt, xt_out, io_sem.at[0]),
        pltpu.make_async_copy(of, og_out, io_sem.at[1]),
    ]
    start(outs)
    z_end()
    swap(1).wait_recv()
    keep[...] = chip_sum(1, 0)
    for d in range(1, planes):
        parts[d - 1][...] = chip_sum(1, d).astype(jnp.bfloat16)

    def drain(p, carry):
        for par in range(2):
            i = 2 * p + par
            for d in range(1, n):
                for kind in range(2):
                    first_send(kind, par, i, d).wait_send()
                    second_send(kind, par, i, d).wait_send()
                    spread_first(kind, par, i, d).wait_send()
                    spread_second(kind, par, i, d).wait_send()
            wait(store(i))
        store_h(2 * p).wait()
        return carry

    lax.fori_loop(0, pairs, drain, 0)
    gather_drain(0, x_ref, xf)
    gather_drain(1, og_ref, of)
    wait(outs)
    for a in range(2):
        swap(a).wait_send()
    for d in range(1, planes):
        z_copy(d).wait_send()


def mix(mesh, inputs, gate_weight, up_weight, down_weight, out_grad):
    rows, cols = mesh.shape["row"], mesh.shape["col"]
    n = math.isqrt(rows)
    assert n * n == rows and cols % 2 == 0
    planes = cols // 2
    tokens, width = inputs.shape[0] * cols, inputs.shape[1]
    hidden = gate_weight.shape[1]
    units = units_of(hidden)
    u = hidden // units
    tb = tokens // rows
    share = tokens // cols
    bf, f32 = jnp.bfloat16, jnp.float32
    dma = pltpu.SemaphoreType.DMA
    vmem = pl.BlockSpec(memory_space=pltpu.VMEM)
    hbm = pl.BlockSpec(memory_space=pl.ANY)
    flops = 12 * tokens * width * hidden
    return pl.pallas_call(
        functools.partial(mix_kernel, n, planes, units),
        out_shape=(
            jax.ShapeDtypeStruct((width, tokens), bf),
            jax.ShapeDtypeStruct((tokens, width), bf),
            jax.ShapeDtypeStruct((hidden, tokens), bf),
            jax.ShapeDtypeStruct((tokens, hidden), bf),
            jax.ShapeDtypeStruct((tokens, hidden), bf),
            jax.ShapeDtypeStruct((share, width), f32),
            jax.ShapeDtypeStruct((share, width), f32),
        )
        + (jax.ShapeDtypeStruct((share, width), bf),) * (planes - 1),
        in_specs=[vmem, vmem, hbm, hbm, hbm],
        out_specs=(hbm, hbm, hbm, hbm, hbm, vmem, vmem) + (vmem,) * (planes - 1),
        scratch_shapes=[
            pltpu.VMEM((tokens, width), bf),
            pltpu.VMEM((tokens, width), bf),
            pltpu.VMEM((RING, 2, width, u), bf),
            pltpu.VMEM((RING, u, width), bf),
            pltpu.VMEM((units, rows, 2, tb, u), bf),
            pltpu.VMEM((units, rows, 1, tb, u), bf),
            pltpu.VMEM((units, n, 2, tb, u), f32),
            pltpu.VMEM((units, n, 1, tb, u), f32),
            pltpu.VMEM((units, n - 1, n, 2, tb, u), bf),
            pltpu.VMEM((units, n - 1, n, 1, tb, u), bf),
            pltpu.VMEM((units, n - 1, 2, tb, u), bf),
            pltpu.VMEM((units, n - 1, 1, tb, u), bf),
            pltpu.VMEM((units, n - 1, 2, tb, u), bf),
            pltpu.VMEM((units, n - 1, 1, tb, u), bf),
            pltpu.VMEM((units, rows, 1, tb, u), bf),
            pltpu.VMEM((units, rows, 2, tb, u), bf),
            pltpu.VMEM((width, tokens), bf),
            pltpu.VMEM((hidden, tokens), bf),
            pltpu.VMEM((tokens, 2 * u), bf),
            pltpu.VMEM((2, tokens, hidden), bf),
            pltpu.VMEM((2, rows, tb, u), f32),
            pltpu.VMEM((tokens, width), f32),
            pltpu.VMEM((tokens, width), f32),
            pltpu.VMEM((2, planes, share, width), bf),
            pltpu.VMEM((2, planes, share, width), bf),
            pltpu.VMEM((planes - 1, share, width), bf),
            pltpu.VMEM((planes - 1, share, width), bf),
            dma((2, planes - 1)),
            dma((2, planes - 1)),
            dma((2, planes)),
            dma((2, planes)),
            dma((8, units, n - 1)),
            dma((8, units, n - 1)),
            dma((RING, 2)),
            dma((RING,)),
            dma((2,)),
            dma((3, units)),
            dma((2,)),
            dma((2,)),
            dma((planes - 1,)),
            dma((planes - 1,)),
        ],
        compiler_params=pltpu.CompilerParams(
            collective_id=0, has_side_effects=True, vmem_limit_bytes=60 * 2**20
        ),
        cost_estimate=pl.CostEstimate(
            flops=flops, bytes_accessed=12 * width * hidden, transcendentals=0
        ),
    )(inputs, out_grad, gate_weight, up_weight, down_weight)


def grads_kernel(first, xt_ref, gp_ref, up_ref, ht_ref, og_ref, gate_ref, up_out, down_ref):
    step = pl.program_id(0)

    def fill(left, right, out):
        rows = out.shape[0] // 4
        for t in range(4):
            part = slice(t * rows, (t + 1) * rows)
            out[part, :] = jnp.dot(
                left[part, :], right[...], preferred_element_type=jnp.float32
            ).astype(out.dtype)

    @pl.when(step < first)
    def _():
        fill(xt_ref, gp_ref, gate_ref)
        fill(xt_ref, up_ref, up_out)

    @pl.when(step >= first)
    def _():
        fill(ht_ref, og_ref, down_ref)


def weight_grads(inputs_t, gate_part, up_part, hidden_t, out_grad):
    width, tokens = inputs_t.shape
    units = hidden_t.shape[0]
    wide = 512 if units % 512 == 0 else 256
    tall = 512 if width % 512 == 0 else 256
    first, second = units // wide, width // tall
    bf = jnp.bfloat16
    whole = functools.partial(pl.BlockSpec, index_map=lambda i: (0, 0))

    def early(i):
        return (0, jnp.minimum(i, first - 1))

    def late(i):
        return (0, jnp.maximum(i - first, 0))

    return pl.pallas_call(
        functools.partial(grads_kernel, first),
        grid=(first + second,),
        out_shape=(
            jax.ShapeDtypeStruct((width, units), bf),
            jax.ShapeDtypeStruct((width, units), bf),
            jax.ShapeDtypeStruct((units, width), bf),
        ),
        in_specs=[
            whole((width, tokens)),
            pl.BlockSpec((tokens, wide), early),
            pl.BlockSpec((tokens, wide), early),
            whole((units, tokens)),
            pl.BlockSpec((tokens, tall), late),
        ],
        out_specs=(
            pl.BlockSpec((width, wide), early),
            pl.BlockSpec((width, wide), early),
            pl.BlockSpec((units, tall), late),
        ),
        compiler_params=pltpu.CompilerParams(vmem_limit_bytes=60 * 2**20),
        cost_estimate=pl.CostEstimate(
            flops=6 * tokens * width * units,
            bytes_accessed=6 * width * units,
            transcendentals=0,
        ),
    )(inputs_t, gate_part, up_part, hidden_t, out_grad)


def on_device(mesh, inputs, gate_weight, up_weight, down_weight, out_grad):
    inputs_t, all_grads, hidden_t, gate_part, up_part, output, keep, *parts = mix(
        mesh, inputs, gate_weight, up_weight, down_weight, out_grad
    )
    cols = mesh.shape["col"]
    arrived = [
        lax.ppermute(part, "col", [(c, (c + 2 * d + 2) % cols) for c in range(cols)])
        for d, part in enumerate(parts)
    ]
    gate_grad, up_grad, down_grad = weight_grads(
        inputs_t, gate_part, up_part, hidden_t, all_grads
    )
    total = keep
    for part in arrived:
        total = total + part.astype(jnp.float32)
    return (output.astype(jnp.bfloat16), total.astype(jnp.bfloat16), gate_grad, up_grad, down_grad)


def solution(mesh):
    in_specs = (P("col", "row"), P("row", "col"), P("row", "col"), P("col", "row"), P("col", "row"))
    out_specs = (
        P("col", "row"),
        P("col", "row"),
        P("row", "col"),
        P("row", "col"),
        P("col", "row"),
    )
    return jax.shard_map(
        functools.partial(on_device, mesh),
        mesh=mesh, in_specs=in_specs, out_specs=out_specs, check_vma=False,
    )
```

```python
import functools
import math

import jax
import jax.numpy as jnp
from jax import lax
from jax.experimental import pallas as pl
from jax.experimental.pallas import tpu as pltpu
from jax.sharding import PartitionSpec as P

MESH = pl.DeviceIdType.MESH
RING = 4
LAG = 2


def contract_first(left, right):
    return lax.dot_general(
        left, right, (((0,), (0,)), ((), ())), preferred_element_type=jnp.float32
    )


def contract_last(left, right):
    return lax.dot_general(
        left, right, (((1,), (1,)), ((), ())), preferred_element_type=jnp.float32
    )


def units_of(hidden_block):
    for units in (14, 28, 2):
        if hidden_block % (units * 128) == 0:
            return units
    return 2


def mix_kernel(
    side, planes, units,
    x_ref, og_ref, wg_ref, wu_ref, wd_ref,
    xt_out, og_out, ht_out, gp_out, up_out, output, keep, *rest,
):
    parts = rest[: planes - 1]
    (xf, of, wgu, wdn, p_gu, p_h, own_gu, own_h, r1_gu, r1_h, p2_gu, p2_h, r2_gu, r2_h,
    full_h, full_g, xt, ht, hp, stage, tmp, acc_out, acc_in, pair_send, pair_recv, z_out, z_in,
    gz_send, gz_recv, gs_send, gs_recv,
    rs_send, rs_recv, ld_gu, ld_d, io_sem, st_sem, pr_send, pr_recv, z_send, z_recv,
     hf_send, hf_recv) = rest[planes - 1 :]
    n, unit = side, wgu.shape[-1]
    owners = n * n
    tokens, width = xf.shape
    token_block = tokens // owners
    share = tokens // (2 * planes)
    pairs = units // 2
    piece, half_block = share // 2, token_block // 2
    per_block = half_block // piece
    row, col = lax.axis_index("row"), lax.axis_index("col")
    my_y, my_x = row // n, row % n
    z, core = col // 2, col % 2
    sibling = (row, z * 2 + (1 - core))

    def along_x(m):
        return (my_y * n + m, col)

    def along_y(m):
        return (m * n + my_x, col)

    firsts = ((my_x, along_x, my_y, along_y), (my_y, along_y, my_x, along_x))

    def slot_of(par, owner):
        oy, ox = owner // n, owner % n
        return ox * n + oy if par == 0 else oy * n + ox

    def plane(d):
        return (z + d) % planes

    partners = [sibling]
    for d in range(1, planes):
        partners.append((row, plane(d) * 2 + core))
    for d in range(1, n):
        partners.append(along_x((my_x + d) % n))
        partners.append(along_y((my_y + d) % n))
    barrier = pltpu.get_barrier_semaphore()
    for partner in partners:
        pl.semaphore_signal(barrier, inc=1, device_id=partner, device_id_type=MESH)

    def columns(k):
        return pl.ds(pl.multiple_of((k % units) * unit, 128), unit)

    def load_gu(k):
        s = k % RING
        return [
            pltpu.make_async_copy(ref.at[:, columns(k)], wgu.at[s, a], ld_gu.at[s, a])
            for a, ref in enumerate((wg_ref, wu_ref))
        ]

    def load_d(k):
        s = k % RING
        return [pltpu.make_async_copy(wd_ref.at[columns(k), :], wdn.at[s], ld_d.at[s])]

    def start(copies):
        for copy in copies:
            copy.start()

    def wait(copies):
        for copy in copies:
            copy.wait()

    for k in range(RING):
        start(load_gu(k))
        start(load_d(k))

    def rows(c, h):
        at = (c // per_block) * token_block + h * half_block + (c % per_block) * piece
        return pl.ds(pl.multiple_of(at, 16), piece)

    def gather_z(a, src, dst, d):
        h = a % 2
        return pltpu.make_async_remote_copy(
            src_ref=src.at[pl.ds(h * piece, piece)], dst_ref=dst.at[rows(col, h)],
            send_sem=gz_send.at[a, d - 1], recv_sem=gz_recv.at[a, d - 1],
            device_id=(row, plane(d) * 2 + core), device_id_type=MESH,
        )

    def gather_s(a, src, dst, d):
        h = a % 2
        c = ((z + planes - d) % planes) * 2 + core
        return pltpu.make_async_remote_copy(
            src_ref=src.at[pl.ds(h * piece, piece)] if d == 0 else dst.at[rows(c, h)],
            dst_ref=dst.at[rows(c, h)],
            send_sem=gs_send.at[a, d], recv_sem=gs_recv.at[a, d],
            device_id=sibling, device_id_type=MESH,
        )

    def gather_start(a, src, dst):
        for d in range(1, planes):
            gather_z(a, src, dst, d).start()
        gather_s(a, src, dst, 0).start()
        dst[rows(col, a % 2), :] = src[pl.ds((a % 2) * piece, piece), :]

    def gather_end(a, src, dst):
        for d in range(1, planes):
            gather_z(a, src, dst, d).wait_recv()
            gather_s(a, src, dst, d).start()
        for d in range(planes):
            gather_s(a, src, dst, d).wait_recv()

    def gather_left(a, src, dst):
        for d in range(1, planes):
            gather_z(a, src, dst, d).wait_send()

    def gather_drain(a, src, dst):
        for d in range(planes):
            gather_s(a, src, dst, d).wait_send()

    def first_send(kind, par, i, d):
        mine, line, _, _ = firsts[par]
        to = (mine + d) % n
        src, dst = ((p_gu, r1_gu), (p_h, r1_h))[kind]
        return pltpu.make_async_remote_copy(
            src_ref=src.at[i, pl.ds(to * n, n)], dst_ref=dst.at[i, d - 1],
            send_sem=rs_send.at[2 * kind, i, d - 1], recv_sem=rs_recv.at[2 * kind, i, d - 1],
            device_id=line(to), device_id_type=MESH,
        )

    def half_send(h, par, i, d):
        mine, line, _, _ = firsts[par]
        to = (mine + d) % n
        part = pl.ds(h * half_block, half_block)
        return pltpu.make_async_remote_copy(
            src_ref=p_gu.at[i, pl.ds(to * n, n), :, part],
            dst_ref=r1_gu.at[i, d - 1, :, :, part],
            send_sem=hf_send.at[h, i, d - 1], recv_sem=hf_recv.at[h, i, d - 1],
            device_id=line(to), device_id_type=MESH,
        )

    def second_send(kind, par, i, d):
        _, _, mine, line = firsts[par]
        src, dst = ((p2_gu, r2_gu), (p2_h, r2_h))[kind]
        return pltpu.make_async_remote_copy(
            src_ref=src.at[i, d - 1], dst_ref=dst.at[i, d - 1],
            send_sem=rs_send.at[2 * kind + 1, i, d - 1],
            recv_sem=rs_recv.at[2 * kind + 1, i, d - 1],
            device_id=line((mine + d) % n), device_id_type=MESH,
        )

    fulls = (full_h, full_g)

    def spread_first(kind, par, i, d):
        mine_f, _, mine_s, line = firsts[par]
        block = fulls[kind].at[i, mine_f * n + mine_s]
        return pltpu.make_async_remote_copy(
            src_ref=block, dst_ref=block,
            send_sem=rs_send.at[4 + 2 * kind, i, d - 1],
            recv_sem=rs_recv.at[4 + 2 * kind, i, d - 1],
            device_id=line((mine_s + d) % n), device_id_type=MESH,
        )

    def spread_second(kind, par, i, d):
        mine, line, _, _ = firsts[par]
        blocks = fulls[kind].at[i, pl.ds(mine * n, n)]
        return pltpu.make_async_remote_copy(
            src_ref=blocks, dst_ref=blocks,
            send_sem=rs_send.at[5 + 2 * kind, i, d - 1],
            recv_sem=rs_recv.at[5 + 2 * kind, i, d - 1],
            device_id=line((mine + d) % n), device_id_type=MESH,
        )

    def put_partial(par, i, a, value, partial, own, arrays):
        mine = firsts[par][0]
        for owner in range(owners):
            block = value[owner * token_block:(owner + 1) * token_block]
            tmp[a, slot_of(par, owner)] = block
            partial[i, slot_of(par, owner), a] = block.astype(jnp.bfloat16)
        for s in range(n):
            own[i, s, a] = tmp[a, mine * n + s]

    def project(par, i):
        s = i % RING
        wait(load_gu(i))
        for a in range(2):
            value = jnp.dot(xf[...], wgu[s, a], preferred_element_type=jnp.float32)
            put_partial(par, i, a, value, p_gu, own_gu, 2)
        start(load_gu(i + RING))
        for d in range(1, n):
            first_send(0, par, i, d).start()

    def project_half(h, par, i):
        mine = firsts[par][0]
        part = pl.ds(h * half_block, half_block)
        left = jnp.concatenate(
            [xf[pl.ds(o * token_block + h * half_block, half_block), :] for o in range(owners)]
        )
        for a in range(2):
            value = jnp.dot(left, wgu[i, a], preferred_element_type=jnp.float32)
            for owner in range(owners):
                block = value[owner * half_block:(owner + 1) * half_block]
                slot = slot_of(par, owner)
                tmp[a, slot, part] = block
                p_gu[i, slot, a, part] = block.astype(jnp.bfloat16)
            for s in range(n):
                own_gu[i, s, a, part] = tmp[a, mine * n + s, part]
        for d in range(1, n):
            half_send(h, par, i, d).start()

    tile = min(512, width)

    def grad_pair(pair):
        i = 2 * pair
        s = i % RING
        for par in range(2):
            wait(load_d(i + par))
            value = contract_last(of[...], wdn[s + par])
            put_partial(par, i + par, 0, value, p_h, own_h, 1)
            for d in range(1, n):
                first_send(1, par, i + par, d).start()
        for par in range(2):
            for d in range(1, n):
                spread_second(0, par, i + par, d).wait_recv()
            for owner in range(owners):
                hp[pl.ds(owner * token_block, token_block), par * unit:(par + 1) * unit] = (
                    full_h[i + par, slot_of(par, owner), 0]
                )
        ht[pl.ds(pl.multiple_of(i * unit, 128), 2 * unit), :] = hp[...].T
        store_h(i).start()

        def add(t, carry):
            cols = pl.ds(pl.multiple_of(t * tile, 128), tile)
            down = wdn[pl.ds(s, 2), :, cols].reshape(2 * unit, tile)
            acc_out[:, cols] += jnp.dot(
                hp[...], down, preferred_element_type=jnp.float32
            )
            return carry

        lax.fori_loop(0, width // tile, add, 0)

        @pl.when(i + RING < units)
        def _():
            for par in range(2):
                start(load_d(i + par + RING))

    def halfway(kind, par, i):
        mine = firsts[par][2]
        own, got, out = ((own_gu, r1_gu, p2_gu), (own_h, r1_h, p2_h))[kind]
        if kind == 0:
            @pl.when(i < RING)
            def _():
                for d in range(1, n):
                    for h in range(2):
                        half_send(h, par, i, d).wait_recv()

            @pl.when(i >= RING)
            def _():
                for d in range(1, n):
                    first_send(kind, par, i, d).wait_recv()
        else:
            for d in range(1, n):
                first_send(kind, par, i, d).wait_recv()
        for d in range(1, n):
            s = (mine + d) % n
            for a in range(2 - kind):
                total = own[i, s, a]
                for e in range(n - 1):
                    total = total + got[i, e, s, a].astype(jnp.float32)
                out[i, d - 1, a] = total.astype(jnp.bfloat16)
            second_send(kind, par, i, d).start()

    def total_of(kind, par, i, a):
        mine = firsts[par][2]
        own, got, last = ((own_gu, r1_gu, r2_gu), (own_h, r1_h, r2_h))[kind]
        total = own[i, mine, a]
        for e in range(n - 1):
            total = total + got[i, e, mine, a].astype(jnp.float32)
        for e in range(n - 1):
            total = total + last[i, e, a].astype(jnp.float32)
        return total

    def gate_hidden(par, i):
        for d in range(1, n):
            second_send(0, par, i, d).wait_recv()
        gate_value = total_of(0, par, i, 0)
        up_value = total_of(0, par, i, 1)
        sig = jax.nn.sigmoid(gate_value)
        mine = firsts[par][0] * n + firsts[par][2]
        full_h[i, mine, 0] = (gate_value * sig * up_value).astype(jnp.bfloat16)
        for d in range(1, n):
            spread_first(0, par, i, d).start()

    def gate_grads(par, i):
        for d in range(1, n):
            second_send(1, par, i, d).wait_recv()
        gate_value = total_of(0, par, i, 0)
        up_value = total_of(0, par, i, 1)
        hidden_grad = total_of(1, par, i, 0)
        sig = jax.nn.sigmoid(gate_value)
        mine = firsts[par][0] * n + firsts[par][2]
        slope = sig * (1.0 + gate_value * (1.0 - sig))
        full_g[i, mine, 0] = (hidden_grad * up_value * slope).astype(jnp.bfloat16)
        full_g[i, mine, 1] = (hidden_grad * gate_value * sig).astype(jnp.bfloat16)
        for d in range(1, n):
            spread_first(1, par, i, d).start()

    def forward(kind, par, i):
        for d in range(1, n):
            spread_first(kind, par, i, d).wait_recv()
        for d in range(1, n):
            spread_second(kind, par, i, d).start()

    def store_h(i):
        strip = pl.ds(pl.multiple_of(i * unit, 128), 2 * unit)
        return pltpu.make_async_copy(ht.at[strip], ht_out.at[strip], st_sem.at[2, i])

    def store(i):
        return [
            pltpu.make_async_copy(
                stage.at[a, :, columns(i)], out.at[:, columns(i)], st_sem.at[a, i]
            )
            for a, out in enumerate((gp_out, up_out))
        ]

    def finish(pair):
        i = 2 * pair
        k = units + i
        s = k % RING
        for par in range(2):
            for d in range(1, n):
                spread_second(1, par, i + par, d).wait_recv()
            for a in range(2):
                for owner in range(owners):
                    stage[a, pl.ds(owner * token_block, token_block), columns(i + par)] = full_g[
                        i + par, slot_of(par, owner), a
                    ]
            start(store(i + par))
            wait(load_gu(k + par))

        def add(t, carry):
            cols = pl.ds(pl.multiple_of(t * tile, 128), tile)
            total = acc_in[:, cols]
            for par in range(2):
                for a in range(2):
                    total = total + contract_last(
                        stage[a, :, columns(i + par)], wgu[s + par, a, cols, :]
                    )
            acc_in[:, cols] = total
            return carry

        lax.fori_loop(0, width // tile, add, 0)

        @pl.when(k + RING < 2 * units)
        def _():
            for par in range(2):
                start(load_gu(k + par + RING))

    totals = (acc_out, acc_in)

    def swap(a):
        return pltpu.make_async_remote_copy(
            src_ref=pair_send.at[a], dst_ref=pair_recv.at[a],
            send_sem=pr_send.at[a], recv_sem=pr_recv.at[a],
            device_id=sibling, device_id_type=MESH,
        )

    def swap_start(a):
        for p in range(planes):
            for h in range(2):
                pair_send[a, p, pl.ds(h * piece, piece)] = totals[a][
                    rows(2 * p + 1 - core, h), :
                ].astype(jnp.bfloat16)
        swap(a).start()

    def chip_sum(a, d):
        p = plane(d)
        mine = jnp.concatenate([totals[a][rows(2 * p + core, h), :] for h in range(2)])
        return mine + pair_recv[a, p].astype(jnp.float32)

    def z_copy(d):
        return pltpu.make_async_remote_copy(
            src_ref=z_out.at[d - 1], dst_ref=z_in.at[d - 1],
            send_sem=z_send.at[d - 1], recv_sem=z_recv.at[d - 1],
            device_id=(row, plane(d) * 2 + core), device_id_type=MESH,
        )

    def z_start():
        swap(0).wait_recv()
        for d in range(1, planes):
            z_out[d - 1] = chip_sum(0, d).astype(jnp.bfloat16)
            z_copy(d).start()

    def z_end():
        total = chip_sum(0, 0)
        for d in range(1, planes):
            z_copy(d).wait_recv()
            total = total + z_in[d - 1].astype(jnp.float32)
        output[...] = total

    pl.semaphore_wait(barrier, len(partners))
    gather_start(0, x_ref, xf)
    gather_left(0, x_ref, xf)
    gather_start(1, x_ref, xf)
    acc_out[...] = jnp.zeros_like(acc_out)
    acc_in[...] = jnp.zeros_like(acc_in)
    for h in range(2):
        gather_end(h, x_ref, xf)
        if h == 1:
            gather_left(1, x_ref, xf)
            gather_start(2, og_ref, of)
            gather_start(3, og_ref, of)

        def early(p, carry):
            for par in range(2):
                i = 2 * p + par
                if h == 0:
                    wait(load_gu(i))
                project_half(h, par, i)
                if h == 1:
                    start(load_gu(i + RING))
            return carry

        lax.fori_loop(0, RING // 2, early, 0)

    starts = {}
    starts["project"] = 0
    starts["halfway0"] = LAG
    starts["hidden"] = 2 * LAG
    starts["spread0"] = 2 * LAG + 1
    starts["grad"] = pairs
    starts["halfway1"] = pairs + LAG
    starts["grads"] = pairs + 2 * LAG
    starts["spread1"] = starts["grads"] + 1
    starts["finish"] = starts["grads"] + 2
    steps = starts["finish"] + pairs

    def step(t, carry):
        def during(name, work):
            first = starts[name]

            @pl.when(jnp.logical_and(t >= first, t < first + pairs))
            def _():
                for par in range(2):
                    work(par, 2 * (t - first) + par)

        @pl.when(t == pairs)
        def _():
            gather_end(2, og_ref, of)
            gather_end(3, og_ref, of)
            for c in range(0, width, 256):
                xt[c:c + 256, :] = xf[:, c:c + 256].T

        during("project", project)
        during("halfway0", functools.partial(halfway, 0))
        during("hidden", gate_hidden)
        during("spread0", functools.partial(forward, 0))

        @pl.when(jnp.logical_and(t >= pairs, t < 2 * pairs))
        def _():
            grad_pair(t - pairs)

        during("halfway1", functools.partial(halfway, 1))
        during("grads", gate_grads)
        during("spread1", functools.partial(forward, 1))

        @pl.when(t == 2 * pairs)
        def _():
            swap_start(0)

        @pl.when(t == 2 * pairs + 1)
        def _():
            z_start()

        @pl.when(t >= starts["finish"])
        def _():
            finish(t - starts["finish"])

        return carry

    lax.fori_loop(RING // 2, steps, step, 0)

    swap_start(1)
    outs = [
        pltpu.make_async_copy(xt, xt_out, io_sem.at[0]),
        pltpu.make_async_copy(of, og_out, io_sem.at[1]),
    ]
    start(outs)
    z_end()
    swap(1).wait_recv()
    keep[...] = chip_sum(1, 0)
    for d in range(1, planes):
        parts[d - 1][...] = chip_sum(1, d).astype(jnp.bfloat16)

    def drain(p, carry):
        for par in range(2):
            i = 2 * p + par
            for d in range(1, n):
                first_send(1, par, i, d).wait_send()

                @pl.when(i < RING)
                def _():
                    for h in range(2):
                        half_send(h, par, i, d).wait_send()

                @pl.when(i >= RING)
                def _():
                    first_send(0, par, i, d).wait_send()

                for kind in range(2):
                    second_send(kind, par, i, d).wait_send()
                    spread_first(kind, par, i, d).wait_send()
                    spread_second(kind, par, i, d).wait_send()
            wait(store(i))
        store_h(2 * p).wait()
        return carry

    lax.fori_loop(0, pairs, drain, 0)
    gather_drain(0, x_ref, xf)
    gather_drain(1, x_ref, xf)
    for a in (2, 3):
        gather_left(a, og_ref, of)
        gather_drain(a, og_ref, of)
    wait(outs)
    for a in range(2):
        swap(a).wait_send()
    for d in range(1, planes):
        z_copy(d).wait_send()


def mix(mesh, inputs, gate_weight, up_weight, down_weight, out_grad):
    rows, cols = mesh.shape["row"], mesh.shape["col"]
    n = math.isqrt(rows)
    assert n * n == rows and cols % 2 == 0
    planes = cols // 2
    tokens, width = inputs.shape[0] * cols, inputs.shape[1]
    hidden = gate_weight.shape[1]
    units = units_of(hidden)
    u = hidden // units
    tb = tokens // rows
    share = tokens // cols
    bf, f32 = jnp.bfloat16, jnp.float32
    dma = pltpu.SemaphoreType.DMA
    vmem = pl.BlockSpec(memory_space=pltpu.VMEM)
    hbm = pl.BlockSpec(memory_space=pl.ANY)
    flops = 12 * tokens * width * hidden
    return pl.pallas_call(
        functools.partial(mix_kernel, n, planes, units),
        out_shape=(
            jax.ShapeDtypeStruct((width, tokens), bf),
            jax.ShapeDtypeStruct((tokens, width), bf),
            jax.ShapeDtypeStruct((hidden, tokens), bf),
            jax.ShapeDtypeStruct((tokens, hidden), bf),
            jax.ShapeDtypeStruct((tokens, hidden), bf),
            jax.ShapeDtypeStruct((share, width), f32),
            jax.ShapeDtypeStruct((share, width), f32),
        )
        + (jax.ShapeDtypeStruct((share, width), bf),) * (planes - 1),
        in_specs=[vmem, vmem, hbm, hbm, hbm],
        out_specs=(hbm, hbm, hbm, hbm, hbm, vmem, vmem) + (vmem,) * (planes - 1),
        scratch_shapes=[
            pltpu.VMEM((tokens, width), bf),
            pltpu.VMEM((tokens, width), bf),
            pltpu.VMEM((RING, 2, width, u), bf),
            pltpu.VMEM((RING, u, width), bf),
            pltpu.VMEM((units, rows, 2, tb, u), bf),
            pltpu.VMEM((units, rows, 1, tb, u), bf),
            pltpu.VMEM((units, n, 2, tb, u), f32),
            pltpu.VMEM((units, n, 1, tb, u), f32),
            pltpu.VMEM((units, n - 1, n, 2, tb, u), bf),
            pltpu.VMEM((units, n - 1, n, 1, tb, u), bf),
            pltpu.VMEM((units, n - 1, 2, tb, u), bf),
            pltpu.VMEM((units, n - 1, 1, tb, u), bf),
            pltpu.VMEM((units, n - 1, 2, tb, u), bf),
            pltpu.VMEM((units, n - 1, 1, tb, u), bf),
            pltpu.VMEM((units, rows, 1, tb, u), bf),
            pltpu.VMEM((units, rows, 2, tb, u), bf),
            pltpu.VMEM((width, tokens), bf),
            pltpu.VMEM((hidden, tokens), bf),
            pltpu.VMEM((tokens, 2 * u), bf),
            pltpu.VMEM((2, tokens, hidden), bf),
            pltpu.VMEM((2, rows, tb, u), f32),
            pltpu.VMEM((tokens, width), f32),
            pltpu.VMEM((tokens, width), f32),
            pltpu.VMEM((2, planes, share, width), bf),
            pltpu.VMEM((2, planes, share, width), bf),
            pltpu.VMEM((planes - 1, share, width), bf),
            pltpu.VMEM((planes - 1, share, width), bf),
            dma((4, planes - 1)),
            dma((4, planes - 1)),
            dma((4, planes)),
            dma((4, planes)),
            dma((8, units, n - 1)),
            dma((8, units, n - 1)),
            dma((RING, 2)),
            dma((RING,)),
            dma((2,)),
            dma((3, units)),
            dma((2,)),
            dma((2,)),
            dma((planes - 1,)),
            dma((planes - 1,)),
            dma((2, RING, n - 1)),
            dma((2, RING, n - 1)),
        ],
        compiler_params=pltpu.CompilerParams(
            collective_id=0, has_side_effects=True, vmem_limit_bytes=60 * 2**20
        ),
        cost_estimate=pl.CostEstimate(
            flops=flops, bytes_accessed=12 * width * hidden, transcendentals=0
        ),
    )(inputs, out_grad, gate_weight, up_weight, down_weight)


def grads_kernel(first, xt_ref, gp_ref, up_ref, ht_ref, og_ref, gate_ref, up_out, down_ref):
    step = pl.program_id(0)

    def fill(left, right, out):
        rows = out.shape[0] // 4
        for t in range(4):
            part = slice(t * rows, (t + 1) * rows)
            out[part, :] = jnp.dot(
                left[part, :], right[...], preferred_element_type=jnp.float32
            ).astype(out.dtype)

    @pl.when(step < first)
    def _():
        fill(xt_ref, gp_ref, gate_ref)
        fill(xt_ref, up_ref, up_out)

    @pl.when(step >= first)
    def _():
        fill(ht_ref, og_ref, down_ref)


def weight_grads(inputs_t, gate_part, up_part, hidden_t, out_grad):
    width, tokens = inputs_t.shape
    units = hidden_t.shape[0]
    wide = 512 if units % 512 == 0 else 256
    tall = 512 if width % 512 == 0 else 256
    first, second = units // wide, width // tall
    bf = jnp.bfloat16
    whole = functools.partial(pl.BlockSpec, index_map=lambda i: (0, 0))

    def early(i):
        return (0, jnp.minimum(i, first - 1))

    def late(i):
        return (0, jnp.maximum(i - first, 0))

    return pl.pallas_call(
        functools.partial(grads_kernel, first),
        grid=(first + second,),
        out_shape=(
            jax.ShapeDtypeStruct((width, units), bf),
            jax.ShapeDtypeStruct((width, units), bf),
            jax.ShapeDtypeStruct((units, width), bf),
        ),
        in_specs=[
            whole((width, tokens)),
            pl.BlockSpec((tokens, wide), early),
            pl.BlockSpec((tokens, wide), early),
            whole((units, tokens)),
            pl.BlockSpec((tokens, tall), late),
        ],
        out_specs=(
            pl.BlockSpec((width, wide), early),
            pl.BlockSpec((width, wide), early),
            pl.BlockSpec((units, tall), late),
        ),
        compiler_params=pltpu.CompilerParams(vmem_limit_bytes=60 * 2**20),
        cost_estimate=pl.CostEstimate(
            flops=6 * tokens * width * units,
            bytes_accessed=6 * width * units,
            transcendentals=0,
        ),
    )(inputs_t, gate_part, up_part, hidden_t, out_grad)


def on_device(mesh, inputs, gate_weight, up_weight, down_weight, out_grad):
    inputs_t, all_grads, hidden_t, gate_part, up_part, output, keep, *parts = mix(
        mesh, inputs, gate_weight, up_weight, down_weight, out_grad
    )
    cols = mesh.shape["col"]
    arrived = [
        lax.ppermute(part, "col", [(c, (c + 2 * d + 2) % cols) for c in range(cols)])
        for d, part in enumerate(parts)
    ]
    gate_grad, up_grad, down_grad = weight_grads(
        inputs_t, gate_part, up_part, hidden_t, all_grads
    )
    total = keep
    for part in arrived:
        total = total + part.astype(jnp.float32)
    return (output.astype(jnp.bfloat16), total.astype(jnp.bfloat16), gate_grad, up_grad, down_grad)


def solution(mesh):
    in_specs = (P("col", "row"), P("row", "col"), P("row", "col"), P("col", "row"), P("col", "row"))
    out_specs = (
        P("col", "row"),
        P("col", "row"),
        P("row", "col"),
        P("row", "col"),
        P("col", "row"),
    )
    return jax.shard_map(
        functools.partial(on_device, mesh),
        mesh=mesh, in_specs=in_specs, out_specs=out_specs, check_vma=False,
    )
```

```python
import functools
import math

import jax
import jax.numpy as jnp
from jax import lax
from jax.experimental import pallas as pl
from jax.experimental.pallas import tpu as pltpu
from jax.sharding import PartitionSpec as P

MESH = pl.DeviceIdType.MESH
RING = 4


def contract_first(left, right):
    return lax.dot_general(
        left, right, (((0,), (0,)), ((), ())), preferred_element_type=jnp.float32
    )


def contract_last(left, right):
    return lax.dot_general(
        left, right, (((1,), (1,)), ((), ())), preferred_element_type=jnp.float32
    )


def units_of(hidden_block):
    for units in (14, 28, 2):
        if hidden_block % (units * 128) == 0:
            return units
    return 2


def mix_kernel(
    side, planes, units,
    x_ref, og_ref, wg_ref, wu_ref, wd_ref,
    xt_out, og_out, ht_out, gp_out, up_out, output, keep, *rest,
):
    parts = rest[: planes - 1]
    (xf, of, wgu, wdn, p_gu, p_h, own_gu, own_h, r1_gu, r1_h, p2_gu, p2_h, r2_gu, r2_h,
    full_h, full_g, xt, ht, hp, stage, tmp, acc_out, acc_in, pair_send, pair_recv, z_out, z_in,
    gz_send, gz_recv, gs_send, gs_recv,
    rs_send, rs_recv, ld_gu, ld_d, io_sem, st_sem, pr_send, pr_recv, z_send, z_recv,
     hf_send, hf_recv) = rest[planes - 1 :]
    n, unit = side, wgu.shape[-1]
    owners = n * n
    tokens, width = xf.shape
    token_block = tokens // owners
    share = tokens // (2 * planes)
    pairs = units // 2
    piece, half_block = share // 2, token_block // 2
    per_block = half_block // piece
    row, col = lax.axis_index("row"), lax.axis_index("col")
    my_y, my_x = row // n, row % n
    z, core = col // 2, col % 2
    sibling = (row, z * 2 + (1 - core))

    def along_x(m):
        return (my_y * n + m, col)

    def along_y(m):
        return (m * n + my_x, col)

    firsts = ((my_x, along_x, my_y, along_y), (my_y, along_y, my_x, along_x))

    def slot_of(par, owner):
        oy, ox = owner // n, owner % n
        return ox * n + oy if par == 0 else oy * n + ox

    def plane(d):
        return (z + d) % planes

    partners = [sibling]
    for d in range(1, planes):
        partners.append((row, plane(d) * 2 + core))
    for d in range(1, n):
        partners.append(along_x((my_x + d) % n))
        partners.append(along_y((my_y + d) % n))
    barrier = pltpu.get_barrier_semaphore()
    for partner in partners:
        pl.semaphore_signal(barrier, inc=1, device_id=partner, device_id_type=MESH)

    def columns(k):
        return pl.ds(pl.multiple_of((k % units) * unit, 128), unit)

    def load_gu(k):
        s = k % RING
        return [
            pltpu.make_async_copy(ref.at[:, columns(k)], wgu.at[s, a], ld_gu.at[s, a])
            for a, ref in enumerate((wg_ref, wu_ref))
        ]

    def load_d(k):
        s = k % RING
        return [pltpu.make_async_copy(wd_ref.at[columns(k), :], wdn.at[s], ld_d.at[s])]

    def start(copies):
        for copy in copies:
            copy.start()

    def wait(copies):
        for copy in copies:
            copy.wait()

    for k in range(RING):
        start(load_gu(k))
        start(load_d(k))

    def rows(c, h):
        at = (c // per_block) * token_block + h * half_block + (c % per_block) * piece
        return pl.ds(pl.multiple_of(at, 16), piece)

    def gather_z(a, src, dst, d):
        h = a % 2
        return pltpu.make_async_remote_copy(
            src_ref=src.at[pl.ds(h * piece, piece)], dst_ref=dst.at[rows(col, h)],
            send_sem=gz_send.at[a, d - 1], recv_sem=gz_recv.at[a, d - 1],
            device_id=(row, plane(d) * 2 + core), device_id_type=MESH,
        )

    def gather_s(a, src, dst, d):
        h = a % 2
        c = ((z + planes - d) % planes) * 2 + core
        return pltpu.make_async_remote_copy(
            src_ref=src.at[pl.ds(h * piece, piece)] if d == 0 else dst.at[rows(c, h)],
            dst_ref=dst.at[rows(c, h)],
            send_sem=gs_send.at[a, d], recv_sem=gs_recv.at[a, d],
            device_id=sibling, device_id_type=MESH,
        )

    def gather_start(a, src, dst):
        for d in range(1, planes):
            gather_z(a, src, dst, d).start()
        gather_s(a, src, dst, 0).start()
        dst[rows(col, a % 2), :] = src[pl.ds((a % 2) * piece, piece), :]

    def gather_end(a, src, dst):
        for d in range(1, planes):
            gather_z(a, src, dst, d).wait_recv()
            gather_s(a, src, dst, d).start()
        for d in range(planes):
            gather_s(a, src, dst, d).wait_recv()

    def gather_left(a, src, dst):
        for d in range(1, planes):
            gather_z(a, src, dst, d).wait_send()

    def gather_drain(a, src, dst):
        for d in range(planes):
            gather_s(a, src, dst, d).wait_send()

    def first_send(kind, par, i, d):
        mine, line, _, _ = firsts[par]
        to = (mine + d) % n
        src, dst = ((p_gu, r1_gu), (p_h, r1_h))[kind]
        return pltpu.make_async_remote_copy(
            src_ref=src.at[i, pl.ds(to * n, n)], dst_ref=dst.at[i, d - 1],
            send_sem=rs_send.at[2 * kind, i, d - 1], recv_sem=rs_recv.at[2 * kind, i, d - 1],
            device_id=line(to), device_id_type=MESH,
        )

    def half_send(h, par, i, d):
        mine, line, _, _ = firsts[par]
        to = (mine + d) % n
        part = pl.ds(h * half_block, half_block)
        return pltpu.make_async_remote_copy(
            src_ref=p_gu.at[i, pl.ds(to * n, n), :, part],
            dst_ref=r1_gu.at[i, d - 1, :, :, part],
            send_sem=hf_send.at[h, i, d - 1], recv_sem=hf_recv.at[h, i, d - 1],
            device_id=line(to), device_id_type=MESH,
        )

    def second_send(kind, par, i, d):
        _, _, mine, line = firsts[par]
        src, dst = ((p2_gu, r2_gu), (p2_h, r2_h))[kind]
        return pltpu.make_async_remote_copy(
            src_ref=src.at[i, d - 1], dst_ref=dst.at[i, d - 1],
            send_sem=rs_send.at[2 * kind + 1, i, d - 1],
            recv_sem=rs_recv.at[2 * kind + 1, i, d - 1],
            device_id=line((mine + d) % n), device_id_type=MESH,
        )

    fulls = (full_h, full_g)

    def spread_first(kind, par, i, d):
        mine_f, _, mine_s, line = firsts[par]
        block = fulls[kind].at[i, mine_f * n + mine_s]
        return pltpu.make_async_remote_copy(
            src_ref=block, dst_ref=block,
            send_sem=rs_send.at[4 + 2 * kind, i, d - 1],
            recv_sem=rs_recv.at[4 + 2 * kind, i, d - 1],
            device_id=line((mine_s + d) % n), device_id_type=MESH,
        )

    def spread_second(kind, par, i, d):
        mine, line, _, _ = firsts[par]
        blocks = fulls[kind].at[i, pl.ds(mine * n, n)]
        return pltpu.make_async_remote_copy(
            src_ref=blocks, dst_ref=blocks,
            send_sem=rs_send.at[5 + 2 * kind, i, d - 1],
            recv_sem=rs_recv.at[5 + 2 * kind, i, d - 1],
            device_id=line((mine + d) % n), device_id_type=MESH,
        )

    def put_partial(par, i, a, value, partial, own, arrays):
        mine = firsts[par][0]
        for owner in range(owners):
            block = value[owner * token_block:(owner + 1) * token_block]
            tmp[a, slot_of(par, owner)] = block
            partial[i, slot_of(par, owner), a] = block.astype(jnp.bfloat16)
        for s in range(n):
            own[i, s, a] = tmp[a, mine * n + s]

    def project(par, i):
        s = i % RING
        wait(load_gu(i))
        for a in range(2):
            value = jnp.dot(xf[...], wgu[s, a], preferred_element_type=jnp.float32)
            put_partial(par, i, a, value, p_gu, own_gu, 2)
        start(load_gu(i + RING))
        for d in range(1, n):
            first_send(0, par, i, d).start()

    def project_half(h, par, i):
        mine = firsts[par][0]
        part = pl.ds(h * half_block, half_block)
        left = jnp.concatenate(
            [xf[pl.ds(o * token_block + h * half_block, half_block), :] for o in range(owners)]
        )
        for a in range(2):
            value = jnp.dot(left, wgu[i, a], preferred_element_type=jnp.float32)
            for owner in range(owners):
                block = value[owner * half_block:(owner + 1) * half_block]
                slot = slot_of(par, owner)
                tmp[a, slot, part] = block
                p_gu[i, slot, a, part] = block.astype(jnp.bfloat16)
            for s in range(n):
                own_gu[i, s, a, part] = tmp[a, mine * n + s, part]
        for d in range(1, n):
            half_send(h, par, i, d).start()

    tile = min(512, width)

    def grad_pair(pair):
        i = 2 * pair
        s = i % RING
        for par in range(2):
            wait(load_d(i + par))
            value = contract_last(of[...], wdn[s + par])
            put_partial(par, i + par, 0, value, p_h, own_h, 1)
            for d in range(1, n):
                first_send(1, par, i + par, d).start()
        for par in range(2):
            for d in range(1, n):
                spread_second(0, par, i + par, d).wait_recv()
            for owner in range(owners):
                hp[pl.ds(owner * token_block, token_block), par * unit:(par + 1) * unit] = (
                    full_h[i + par, slot_of(par, owner), 0]
                )
        ht[pl.ds(pl.multiple_of(i * unit, 128), 2 * unit), :] = hp[...].T
        store_h(i).start()

        def add(t, carry):
            cols = pl.ds(pl.multiple_of(t * tile, 128), tile)
            down = wdn[pl.ds(s, 2), :, cols].reshape(2 * unit, tile)
            acc_out[:, cols] += jnp.dot(
                hp[...], down, preferred_element_type=jnp.float32
            )
            return carry

        lax.fori_loop(0, width // tile, add, 0)

        @pl.when(i + RING < units)
        def _():
            for par in range(2):
                start(load_d(i + par + RING))

    def halfway(kind, par, i):
        mine = firsts[par][2]
        own, got, out = ((own_gu, r1_gu, p2_gu), (own_h, r1_h, p2_h))[kind]
        if kind == 0:
            @pl.when(i < RING)
            def _():
                for d in range(1, n):
                    for h in range(2):
                        half_send(h, par, i, d).wait_recv()

            @pl.when(i >= RING)
            def _():
                for d in range(1, n):
                    first_send(kind, par, i, d).wait_recv()
        else:
            for d in range(1, n):
                first_send(kind, par, i, d).wait_recv()
        for d in range(1, n):
            s = (mine + d) % n
            for a in range(2 - kind):
                total = own[i, s, a]
                for e in range(n - 1):
                    total = total + got[i, e, s, a].astype(jnp.float32)
                out[i, d - 1, a] = total.astype(jnp.bfloat16)
            second_send(kind, par, i, d).start()

    def total_of(kind, par, i, a):
        mine = firsts[par][2]
        own, got, last = ((own_gu, r1_gu, r2_gu), (own_h, r1_h, r2_h))[kind]
        total = own[i, mine, a]
        for e in range(n - 1):
            total = total + got[i, e, mine, a].astype(jnp.float32)
        for e in range(n - 1):
            total = total + last[i, e, a].astype(jnp.float32)
        return total

    def gate_hidden(par, i):
        for d in range(1, n):
            second_send(0, par, i, d).wait_recv()
        gate_value = total_of(0, par, i, 0)
        up_value = total_of(0, par, i, 1)
        sig = jax.nn.sigmoid(gate_value)
        mine = firsts[par][0] * n + firsts[par][2]
        full_h[i, mine, 0] = (gate_value * sig * up_value).astype(jnp.bfloat16)
        for d in range(1, n):
            spread_first(0, par, i, d).start()

    def gate_grads(par, i):
        for d in range(1, n):
            second_send(1, par, i, d).wait_recv()
        gate_value = total_of(0, par, i, 0)
        up_value = total_of(0, par, i, 1)
        hidden_grad = total_of(1, par, i, 0)
        sig = jax.nn.sigmoid(gate_value)
        mine = firsts[par][0] * n + firsts[par][2]
        slope = sig * (1.0 + gate_value * (1.0 - sig))
        full_g[i, mine, 0] = (hidden_grad * up_value * slope).astype(jnp.bfloat16)
        full_g[i, mine, 1] = (hidden_grad * gate_value * sig).astype(jnp.bfloat16)
        for d in range(1, n):
            spread_first(1, par, i, d).start()

    def forward(kind, par, i):
        for d in range(1, n):
            spread_first(kind, par, i, d).wait_recv()
        for d in range(1, n):
            spread_second(kind, par, i, d).start()

    def store_h(i):
        strip = pl.ds(pl.multiple_of(i * unit, 128), 2 * unit)
        return pltpu.make_async_copy(ht.at[strip], ht_out.at[strip], st_sem.at[2, i])

    def store(i):
        return [
            pltpu.make_async_copy(
                stage.at[a, :, columns(i)], out.at[:, columns(i)], st_sem.at[a, i]
            )
            for a, out in enumerate((gp_out, up_out))
        ]

    def finish(pair):
        i = 2 * pair
        k = units + i
        s = k % RING
        for par in range(2):
            for d in range(1, n):
                spread_second(1, par, i + par, d).wait_recv()
            for a in range(2):
                for owner in range(owners):
                    stage[a, pl.ds(owner * token_block, token_block), columns(i + par)] = full_g[
                        i + par, slot_of(par, owner), a
                    ]
            start(store(i + par))
            wait(load_gu(k + par))

        def add(t, carry):
            cols = pl.ds(pl.multiple_of(t * tile, 128), tile)
            total = acc_in[:, cols]
            for par in range(2):
                for a in range(2):
                    total = total + contract_last(
                        stage[a, :, columns(i + par)], wgu[s + par, a, cols, :]
                    )
            acc_in[:, cols] = total
            return carry

        lax.fori_loop(0, width // tile, add, 0)

        @pl.when(k + RING < 2 * units)
        def _():
            for par in range(2):
                start(load_gu(k + par + RING))

    totals = (acc_out, acc_in)

    def swap(a):
        return pltpu.make_async_remote_copy(
            src_ref=pair_send.at[a], dst_ref=pair_recv.at[a],
            send_sem=pr_send.at[a], recv_sem=pr_recv.at[a],
            device_id=sibling, device_id_type=MESH,
        )

    def swap_start(a):
        for p in range(planes):
            for h in range(2):
                pair_send[a, p, pl.ds(h * piece, piece)] = totals[a][
                    rows(2 * p + 1 - core, h), :
                ].astype(jnp.bfloat16)
        swap(a).start()

    def chip_sum(a, d):
        p = plane(d)
        mine = jnp.concatenate([totals[a][rows(2 * p + core, h), :] for h in range(2)])
        return mine + pair_recv[a, p].astype(jnp.float32)

    def z_copy(d):
        return pltpu.make_async_remote_copy(
            src_ref=z_out.at[d - 1], dst_ref=z_in.at[d - 1],
            send_sem=z_send.at[d - 1], recv_sem=z_recv.at[d - 1],
            device_id=(row, plane(d) * 2 + core), device_id_type=MESH,
        )

    def z_start():
        swap(0).wait_recv()
        for d in range(1, planes):
            z_out[d - 1] = chip_sum(0, d).astype(jnp.bfloat16)
            z_copy(d).start()

    def z_end():
        total = chip_sum(0, 0)
        for d in range(1, planes):
            z_copy(d).wait_recv()
            total = total + z_in[d - 1].astype(jnp.float32)
        output[...] = total

    pl.semaphore_wait(barrier, len(partners))
    gather_start(0, x_ref, xf)
    gather_left(0, x_ref, xf)
    gather_start(1, x_ref, xf)
    acc_out[...] = jnp.zeros_like(acc_out)
    acc_in[...] = jnp.zeros_like(acc_in)
    for h in range(2):
        gather_end(h, x_ref, xf)
        if h == 1:
            gather_left(1, x_ref, xf)
            gather_start(2, og_ref, of)
            gather_start(3, og_ref, of)

        def early(p, carry):
            for par in range(2):
                i = 2 * p + par
                if h == 0:
                    wait(load_gu(i))
                project_half(h, par, i)
                if h == 1:
                    start(load_gu(i + RING))
            return carry

        lax.fori_loop(0, RING // 2, early, 0)

    starts = {}
    starts["project"] = 0
    starts["halfway0"] = RING // 2
    starts["hidden"] = starts["halfway0"] + 1
    starts["spread0"] = starts["hidden"] + 1
    starts["grad"] = pairs
    starts["halfway1"] = pairs + 1
    starts["grads"] = pairs + 2
    starts["spread1"] = pairs + 3
    starts["finish"] = pairs + 4
    steps = starts["finish"] + pairs

    def step(t, carry):
        def during(name, work):
            first = starts[name]

            @pl.when(jnp.logical_and(t >= first, t < first + pairs))
            def _():
                for par in range(2):
                    work(par, 2 * (t - first) + par)

        @pl.when(t == pairs)
        def _():
            gather_end(2, og_ref, of)
            gather_end(3, og_ref, of)
            for c in range(0, width, 256):
                xt[c:c + 256, :] = xf[:, c:c + 256].T

        during("project", project)
        during("halfway0", functools.partial(halfway, 0))
        during("hidden", gate_hidden)
        during("spread0", functools.partial(forward, 0))

        @pl.when(jnp.logical_and(t >= pairs, t < 2 * pairs))
        def _():
            grad_pair(t - pairs)

        during("halfway1", functools.partial(halfway, 1))
        during("grads", gate_grads)
        during("spread1", functools.partial(forward, 1))

        @pl.when(t == 2 * pairs)
        def _():
            swap_start(0)

        @pl.when(t == 2 * pairs + 1)
        def _():
            z_start()

        @pl.when(t >= starts["finish"])
        def _():
            finish(t - starts["finish"])

        return carry

    lax.fori_loop(RING // 2, steps, step, 0)

    swap_start(1)
    outs = [
        pltpu.make_async_copy(xt, xt_out, io_sem.at[0]),
        pltpu.make_async_copy(of, og_out, io_sem.at[1]),
    ]
    start(outs)
    z_end()
    swap(1).wait_recv()
    keep[...] = chip_sum(1, 0)
    for d in range(1, planes):
        parts[d - 1][...] = chip_sum(1, d).astype(jnp.bfloat16)

    def drain(p, carry):
        for par in range(2):
            i = 2 * p + par
            for d in range(1, n):
                first_send(1, par, i, d).wait_send()

                @pl.when(i < RING)
                def _():
                    for h in range(2):
                        half_send(h, par, i, d).wait_send()

                @pl.when(i >= RING)
                def _():
                    first_send(0, par, i, d).wait_send()

                for kind in range(2):
                    second_send(kind, par, i, d).wait_send()
                    spread_first(kind, par, i, d).wait_send()
                    spread_second(kind, par, i, d).wait_send()
            wait(store(i))
        store_h(2 * p).wait()
        return carry

    lax.fori_loop(0, pairs, drain, 0)
    gather_drain(0, x_ref, xf)
    gather_drain(1, x_ref, xf)
    for a in (2, 3):
        gather_left(a, og_ref, of)
        gather_drain(a, og_ref, of)
    wait(outs)
    for a in range(2):
        swap(a).wait_send()
    for d in range(1, planes):
        z_copy(d).wait_send()


def mix(mesh, inputs, gate_weight, up_weight, down_weight, out_grad):
    rows, cols = mesh.shape["row"], mesh.shape["col"]
    n = math.isqrt(rows)
    assert n * n == rows and cols % 2 == 0
    planes = cols // 2
    tokens, width = inputs.shape[0] * cols, inputs.shape[1]
    hidden = gate_weight.shape[1]
    units = units_of(hidden)
    u = hidden // units
    tb = tokens // rows
    share = tokens // cols
    bf, f32 = jnp.bfloat16, jnp.float32
    dma = pltpu.SemaphoreType.DMA
    vmem = pl.BlockSpec(memory_space=pltpu.VMEM)
    hbm = pl.BlockSpec(memory_space=pl.ANY)
    flops = 12 * tokens * width * hidden
    return pl.pallas_call(
        functools.partial(mix_kernel, n, planes, units),
        out_shape=(
            jax.ShapeDtypeStruct((width, tokens), bf),
            jax.ShapeDtypeStruct((tokens, width), bf),
            jax.ShapeDtypeStruct((hidden, tokens), bf),
            jax.ShapeDtypeStruct((tokens, hidden), bf),
            jax.ShapeDtypeStruct((tokens, hidden), bf),
            jax.ShapeDtypeStruct((share, width), f32),
            jax.ShapeDtypeStruct((share, width), f32),
        )
        + (jax.ShapeDtypeStruct((share, width), bf),) * (planes - 1),
        in_specs=[vmem, vmem, hbm, hbm, hbm],
        out_specs=(hbm, hbm, hbm, hbm, hbm, vmem, vmem) + (vmem,) * (planes - 1),
        scratch_shapes=[
            pltpu.VMEM((tokens, width), bf),
            pltpu.VMEM((tokens, width), bf),
            pltpu.VMEM((RING, 2, width, u), bf),
            pltpu.VMEM((RING, u, width), bf),
            pltpu.VMEM((units, rows, 2, tb, u), bf),
            pltpu.VMEM((units, rows, 1, tb, u), bf),
            pltpu.VMEM((units, n, 2, tb, u), f32),
            pltpu.VMEM((units, n, 1, tb, u), f32),
            pltpu.VMEM((units, n - 1, n, 2, tb, u), bf),
            pltpu.VMEM((units, n - 1, n, 1, tb, u), bf),
            pltpu.VMEM((units, n - 1, 2, tb, u), bf),
            pltpu.VMEM((units, n - 1, 1, tb, u), bf),
            pltpu.VMEM((units, n - 1, 2, tb, u), bf),
            pltpu.VMEM((units, n - 1, 1, tb, u), bf),
            pltpu.VMEM((units, rows, 1, tb, u), bf),
            pltpu.VMEM((units, rows, 2, tb, u), bf),
            pltpu.VMEM((width, tokens), bf),
            pltpu.VMEM((hidden, tokens), bf),
            pltpu.VMEM((tokens, 2 * u), bf),
            pltpu.VMEM((2, tokens, hidden), bf),
            pltpu.VMEM((2, rows, tb, u), f32),
            pltpu.VMEM((tokens, width), f32),
            pltpu.VMEM((tokens, width), f32),
            pltpu.VMEM((2, planes, share, width), bf),
            pltpu.VMEM((2, planes, share, width), bf),
            pltpu.VMEM((planes - 1, share, width), bf),
            pltpu.VMEM((planes - 1, share, width), bf),
            dma((4, planes - 1)),
            dma((4, planes - 1)),
            dma((4, planes)),
            dma((4, planes)),
            dma((8, units, n - 1)),
            dma((8, units, n - 1)),
            dma((RING, 2)),
            dma((RING,)),
            dma((2,)),
            dma((3, units)),
            dma((2,)),
            dma((2,)),
            dma((planes - 1,)),
            dma((planes - 1,)),
            dma((2, RING, n - 1)),
            dma((2, RING, n - 1)),
        ],
        compiler_params=pltpu.CompilerParams(
            collective_id=0, has_side_effects=True, vmem_limit_bytes=60 * 2**20
        ),
        cost_estimate=pl.CostEstimate(
            flops=flops, bytes_accessed=12 * width * hidden, transcendentals=0
        ),
    )(inputs, out_grad, gate_weight, up_weight, down_weight)


def grads_kernel(first, xt_ref, gp_ref, up_ref, ht_ref, og_ref, gate_ref, up_out, down_ref):
    step = pl.program_id(0)

    def fill(left, right, out):
        rows = out.shape[0] // 4
        for t in range(4):
            part = slice(t * rows, (t + 1) * rows)
            out[part, :] = jnp.dot(
                left[part, :], right[...], preferred_element_type=jnp.float32
            ).astype(out.dtype)

    @pl.when(step < first)
    def _():
        fill(xt_ref, gp_ref, gate_ref)
        fill(xt_ref, up_ref, up_out)

    @pl.when(step >= first)
    def _():
        fill(ht_ref, og_ref, down_ref)


def weight_grads(inputs_t, gate_part, up_part, hidden_t, out_grad):
    width, tokens = inputs_t.shape
    units = hidden_t.shape[0]
    wide = 512 if units % 512 == 0 else 256
    tall = 512 if width % 512 == 0 else 256
    first, second = units // wide, width // tall
    bf = jnp.bfloat16
    whole = functools.partial(pl.BlockSpec, index_map=lambda i: (0, 0))

    def early(i):
        return (0, jnp.minimum(i, first - 1))

    def late(i):
        return (0, jnp.maximum(i - first, 0))

    return pl.pallas_call(
        functools.partial(grads_kernel, first),
        grid=(first + second,),
        out_shape=(
            jax.ShapeDtypeStruct((width, units), bf),
            jax.ShapeDtypeStruct((width, units), bf),
            jax.ShapeDtypeStruct((units, width), bf),
        ),
        in_specs=[
            whole((width, tokens)),
            pl.BlockSpec((tokens, wide), early),
            pl.BlockSpec((tokens, wide), early),
            whole((units, tokens)),
            pl.BlockSpec((tokens, tall), late),
        ],
        out_specs=(
            pl.BlockSpec((width, wide), early),
            pl.BlockSpec((width, wide), early),
            pl.BlockSpec((units, tall), late),
        ),
        compiler_params=pltpu.CompilerParams(vmem_limit_bytes=60 * 2**20),
        cost_estimate=pl.CostEstimate(
            flops=6 * tokens * width * units,
            bytes_accessed=6 * width * units,
            transcendentals=0,
        ),
    )(inputs_t, gate_part, up_part, hidden_t, out_grad)


def on_device(mesh, inputs, gate_weight, up_weight, down_weight, out_grad):
    inputs_t, all_grads, hidden_t, gate_part, up_part, output, keep, *parts = mix(
        mesh, inputs, gate_weight, up_weight, down_weight, out_grad
    )
    cols = mesh.shape["col"]
    arrived = [
        lax.ppermute(part, "col", [(c, (c + 2 * d + 2) % cols) for c in range(cols)])
        for d, part in enumerate(parts)
    ]
    gate_grad, up_grad, down_grad = weight_grads(
        inputs_t, gate_part, up_part, hidden_t, all_grads
    )
    total = keep
    for part in arrived:
        total = total + part.astype(jnp.float32)
    return (output.astype(jnp.bfloat16), total.astype(jnp.bfloat16), gate_grad, up_grad, down_grad)


def solution(mesh):
    in_specs = (P("col", "row"), P("row", "col"), P("row", "col"), P("col", "row"), P("col", "row"))
    out_specs = (
        P("col", "row"),
        P("col", "row"),
        P("row", "col"),
        P("row", "col"),
        P("col", "row"),
    )
    return jax.shard_map(
        functools.partial(on_device, mesh),
        mesh=mesh, in_specs=in_specs, out_specs=out_specs, check_vma=False,
    )
```
